512 devices in a mesh: exp: 32 (over y_hi, z, core), pix: 16 (over x, y_lo).
Axes of the slice: x: 4, y: 8 (y_hi: 2, y_lo: 4; y = y_hi * 4 + y_lo), z: 8, core: 2. Of those that a mesh axis runs over, the one named last changes fastest.
Arguments:
- transmission: bfloat16 [16384, 24576], P('exp', 'pix'), may hold values from 0.29882812 to 1
- inverse_var: bfloat16 [16384, 24576], P('exp', 'pix'), may hold values from 0.25 to 4
- pixel_mask: int32 [16384, 192], P('exp', 'pix'), may hold values 0 or 1
- coef: bfloat16 [16384, 256], P('exp'), may hold values from -6 to 6
- basis: bfloat16 [256, 24576], P(None, 'pix'), may hold values from -6 to 6
- coef_tangent: bfloat16 [16384, 256], P('exp', 'pix'), may hold values from -0.375 to 0.375
- basis_tangent: bfloat16 [256, 24576], P('exp', 'pix'), may hold values from -0.375 to 0.375
Outputs:
- coef_grad: float32 [16384, 256], P('exp', 'pix')
- basis_grad: float32 [256, 24576], P('exp', 'pix')
The draws below stay inside these ranges and needn't reach their ends.
All inputs are finite; a program needn't handle non-finite values. No bound on the sum of `pixel_mask` on one device may be relied on, other than what follows from the above.
Results may differ from the reference program's by a relative error of at most 0.0008.
Values may be sent and summed in bfloat16 or wider, within the bound.
No kernel may reach another device: no remote copies, remote signals or barrier semaphores. Data moves between devices by JAX's collectives and lax.ppermute only.
A program may use at most 64 MiB of HBM per device.

```python
import math
import jax
import jax.numpy as jnp
from jax import lax

R = 256
TILE = 128
ED = 512
NE = 16384
NP = 24576


def plant(array, rng, low, high):
    extent = array.shape
    index_at = [jax.random.randint(jax.random.fold_in(rng, axis), (), 0, extent[axis]) for axis in range(len(extent))]
    array = array.at[tuple(index_at)].set(low)
    longest = extent.index(max(extent))
    index_at[longest] = (index_at[longest] + 1) % extent[longest]
    return array.at[tuple(index_at)].set(high)


def strengthened(entries, rng, source, target, shards_of, factor):
    owner, partner = [(jnp.arange(entries.shape[dim]) // (entries.shape[dim] // shards_of)).reshape([-1 if axis == dim else 1 for axis in range(entries.ndim)]) for dim in (source, target)]
    chosen = jax.random.permutation(rng, shards_of)[partner]
    strong = (owner == chosen) | (owner == (partner + shards_of // 2) % shards_of)
    return jnp.where(strong, factor * entries, entries)


def levels(key, dims, split, low, largest):
    loudness = 1.0
    for dim, blocks in split:
        draws = jax.random.uniform(jax.random.fold_in(jax.random.fold_in(key, 6), dim), (blocks,), jnp.float32, low / len(split), largest / len(split))
        loudness = loudness * jnp.repeat(jnp.exp(draws), dims[dim] // blocks).reshape((-1,) + (1,) * (len(dims) - 1 - dim))
    return loudness


def normal_values(own_key, dims, width, limit, cuts=(), dtype=jnp.bfloat16):
    result = jax.random.normal(own_key, dims, jnp.float32) * width
    if len(cuts) > 0:
        result = levels(own_key, dims, cuts, -0.22, 0.18) * result
    return jnp.clip(result, min=-limit, max=limit).astype(dtype)


def bell_draw_with(own_key, shape, width, limit, pieces, heavy, kind=jnp.bfloat16):
    entries = width * jax.random.normal(own_key, shape, jnp.float32)
    if pieces:
        entries = entries * levels(own_key, shape, pieces, -0.22, 0.18)
    return jnp.clip(strengthened(entries, jax.random.fold_in(own_key, 3), *heavy), -limit, limit).astype(kind)


def setup_inputs(seed: int = 0) -> dict:
    streams_of = jax.random.split(jax.random.key(seed), 8)
    transmission = jnp.clip(0.29882812 + 0.7011719 * jax.random.uniform(streams_of[0], (NE, NP), jnp.float32) ** levels(streams_of[0], (NE, NP), ((0, 32), (1, 16)), -0.2, 0.2), 0.29882812, 1.0).astype(jnp.bfloat16)
    inverse_var = jnp.clip(jnp.exp(math.log(4.0) - 2.7725887 * jax.random.uniform(streams_of[1], (NE, NP), jnp.float32) ** levels(streams_of[1], (NE, NP), ((0, 32), (1, 16)), -0.2, 0.2)), 0.25, 4.0).astype(jnp.bfloat16)
    pixel_mask = plant((jax.random.randint(streams_of[2], (NE, NP // TILE), 0, 4) < 3).astype(jnp.int32), jax.random.fold_in(streams_of[2], 1), 0, 1)
    coef = bell_draw_with(streams_of[3], (NE, R), 1.0, 6.0, ((0, 32),), (0, 1, 32, 2.75))
    basis = bell_draw_with(streams_of[4], (R, NP), 1.0, 6.0, ((1, 16),), (1, 0, 16, 2.0))
    coef_tangent = normal_values(streams_of[5], (NE, R), R ** -0.5, 0.375, ((0, 32), (1, 16)))
    basis_tangent = normal_values(streams_of[6], (R, NP), R ** -0.5, 0.375, ((0, 32), (1, 16)))
    return dict(transmission=transmission, inverse_var=inverse_var, pixel_mask=pixel_mask, coef=coef, basis=basis, coef_tangent=coef_tangent, basis_tangent=basis_tangent)


def reference(transmission, inverse_var, pixel_mask, coef, basis, coef_tangent, basis_tangent):
    blocks = NE // ED
    trans_b = transmission.reshape(blocks, ED, NP)
    ivar_b = inverse_var.reshape(blocks, ED, NP)
    mask_b = pixel_mask.reshape(blocks, ED, NP // TILE)
    coef_b = coef.reshape(blocks, ED, R)
    tang_b = coef_tangent.reshape(blocks, ED, R)

    def one_block(total, items):
        trans, ivar, mask, cf, tg = items
        spread = jnp.broadcast_to(mask.astype(jnp.float32)[:, :, None], (ED, NP // TILE, TILE)).reshape(ED, NP)
        tr = trans.astype(jnp.float32)
        weights = tr * tr * ivar.astype(jnp.float32) * spread
        moved = jnp.dot(tg, basis, preferred_element_type=jnp.float32) + jnp.dot(cf, basis_tangent, preferred_element_type=jnp.float32)
        weighted = (weights * moved).astype(jnp.bfloat16)
        cgrad = jnp.dot(weighted, basis.T, preferred_element_type=jnp.float32) / math.sqrt(NP)
        total = total + jnp.dot(cf.T, weighted, preferred_element_type=jnp.float32)
        return (total, cgrad)
    start = jnp.zeros((R, NP), jnp.float32)
    total, cgrads = lax.scan(one_block, start, (trans_b, ivar_b, mask_b, coef_b, tang_b))
    return (cgrads.reshape(NE, R), total / math.sqrt(NE))
```

```python
import math

import jax
import jax.numpy as jnp
from jax import lax
from jax.experimental import pallas as pl
from jax.experimental.pallas import tpu as pltpu
from jax.sharding import Mesh
from jax.sharding import PartitionSpec as P

TILE = 128
BF16, F16, F32 = jnp.bfloat16, jnp.float16, jnp.float32
TOP, STEP, RUNGS = -14, 16, 8
STAGES = (("x", 2), ("yl", 2), ("x", 1), ("yl", 1))


def rung_of(amax):
    return sum(
        (amax < 2.0 ** (15 - TOP - STEP * i)).astype(F32) for i in range(1, RUNGS + 1)
    )


def scale_of(rung, sign):
    scale = jnp.full_like(rung, 2.0 ** (sign * TOP))
    for i in range(1, RUNGS + 1):
        scale = scale * jnp.where(rung >= i, F32(2.0 ** (sign * STEP)), F32(1.0))
    return scale


def partner(value, axis, bit):
    size = lax.axis_size(axis)
    return lax.ppermute(value, axis, [(i, i ^ bit) for i in range(size)])


def upper(axis, bit):
    return (lax.axis_index(axis) & bit) != 0


def in_stage_order(rows, count):
    shape = rows.shape
    cut = rows.reshape(2, 2, 2, 2, count, *shape[1:])
    return cut.transpose(3, 1, 2, 0, *range(4, cut.ndim)).reshape(shape)


def first_kernel(trans_ref, ivar_ref, mask_ref, tangent_ref, basis_ref, weights_ref, moved_ref):
    trans = trans_ref[...].astype(F32)
    weights = trans * trans * ivar_ref[...].astype(F32)
    step = pl.program_id(0)
    tiles = trans.shape[1] // TILE
    lanes = lax.broadcasted_iota(jnp.int32, mask_ref.shape, 1)
    for t in range(tiles):
        here = jnp.where(lanes == step * tiles + t, mask_ref[...], 0.0)
        column = jnp.sum(here, axis=1, keepdims=True)
        weights_ref[:, t * TILE : (t + 1) * TILE] = (
            weights[:, t * TILE : (t + 1) * TILE] * column
        )
    moved_ref[...] = lax.dot_general(
        tangent_ref[...], basis_ref[...], (((0,), (0,)), ((), ())), preferred_element_type=F32
    )


def second_kernel(weights_ref, moved_ref, coef_ref, coef_t_ref, full_ref, basis_ref, coef_out, own_out, other_out):
    moved = moved_ref[...] + jnp.dot(coef_ref[...], full_ref[...], preferred_element_type=F32)
    weighted = (weights_ref[...] * moved).astype(BF16)
    sums = jnp.dot(coef_t_ref[...], weighted, preferred_element_type=F32)
    half = own_out.shape[0]
    own_out[...] = sums[:half]
    other_out[...] = sums[half:]
    term = lax.dot_general(
        basis_ref[...], weighted, (((1,), (1,)), ((), ())), preferred_element_type=F32
    )

    @pl.when(pl.program_id(0) == 0)
    def _():
        coef_out[...] = term

    @pl.when(pl.program_id(0) > 0)
    def _():
        coef_out[...] += term


def pack_kernel(own_ref, other_ref, out_ref):
    total = own_ref[...] + other_ref[...]
    cols = total.shape[1]
    amax = jnp.max(jnp.max(jnp.abs(total), axis=0, keepdims=True), axis=1, keepdims=True)
    rung = rung_of(amax)
    out_ref[:, :cols] = total * scale_of(rung, 1)
    out_ref[:, cols:] = jnp.broadcast_to(rung, (total.shape[0], out_ref.shape[1] - cols))


def unpack_kernel(divisor, in_ref, out_ref):
    cols = out_ref.shape[1]
    total = jnp.zeros(out_ref.shape, F32)
    for i in range(in_ref.shape[0]):
        inverse = scale_of(in_ref[i, :, cols : cols + TILE], -1)
        for t in range(cols // TILE):
            part = slice(t * TILE, (t + 1) * TILE)
            out = in_ref[i, :, part] * inverse
            out_ref[:, part] = out if i == 0 else out_ref[:, part] + out
    out_ref[...] = out_ref[...] * (1.0 / divisor)


def body(transmission, inverse_var, pixel_mask, coef, basis, coef_tangent, basis_tangent):
    rows, cols = transmission.shape
    rank = basis.shape[0]
    mine = rank // 32
    exposures, pixels = rows * 32, cols * 16
    core = lax.axis_index("c")

    spread = jnp.broadcast_to(basis_tangent[None], (16, *basis_tangent.shape))
    arrived = lax.all_to_all(spread, ("yh", "z"), 0, 0, tiled=True)

    tangent = coef_tangent.T
    for axis, bit in STAGES:
        other = partner(tangent, axis, bit)
        up = upper(axis, bit)
        tangent = jnp.concatenate(
            [jnp.where(up, other, tangent), jnp.where(up, tangent, other)], axis=0
        )
    basis_p = in_stage_order(basis, rank // 16)
    coef_t = coef.T.reshape(16, 2, mine, rows).transpose(1, 0, 2, 3).reshape(rank, rows)
    coef_p = coef_t.T
    half = rank // 2
    coef_own = jnp.concatenate(
        [
            lax.dynamic_slice_in_dim(coef_t, core * half, half, 0),
            lax.dynamic_slice_in_dim(coef_t, (1 - core) * half, half, 0),
        ],
        axis=0,
    )

    width = 256
    steps = cols // width
    whole = lambda *shape: pl.BlockSpec(shape, lambda i: (0,) * len(shape))
    tall = lambda n: pl.BlockSpec((n, width), lambda i: (0, i))
    weights, moved = pl.pallas_call(
        first_kernel,
        grid=(steps,),
        in_specs=[tall(rows), tall(rows), whole(rows, cols // TILE), whole(rank, rows), tall(rank)],
        out_specs=[tall(rows), tall(rows)],
        out_shape=[jax.ShapeDtypeStruct((rows, cols), F32)] * 2,
        compiler_params=pltpu.CompilerParams(vmem_limit_bytes=24 << 20),
        cost_estimate=pl.CostEstimate(
            flops=2 * rows * cols * rank, bytes_accessed=12 * rows * cols, transcendentals=0
        ),
    )(transmission, inverse_var, pixel_mask.astype(F32), tangent, basis_p)

    full = lax.all_gather(arrived.reshape(half, cols), "c", axis=0, tiled=True)
    coef_term, own, other = pl.pallas_call(
        second_kernel,
        grid=(steps,),
        in_specs=[
            tall(rows), tall(rows), whole(rows, rank), whole(rank, rows), tall(rank), tall(rank),
        ],
        out_specs=[whole(rank, rows), tall(half), tall(half)],
        out_shape=[
            jax.ShapeDtypeStruct((rank, rows), F32),
            jax.ShapeDtypeStruct((half, cols), F32),
            jax.ShapeDtypeStruct((half, cols), F32),
        ],
        compiler_params=pltpu.CompilerParams(vmem_limit_bytes=24 << 20),
        cost_estimate=pl.CostEstimate(
            flops=6 * rows * cols * rank, bytes_accessed=10 * rows * cols, transcendentals=0
        ),
    )(weights, moved, coef_p, coef_own, full, basis_p)

    other = lax.ppermute(other, "c", [(0, 1), (1, 0)])
    packed = pl.pallas_call(
        pack_kernel, out_shape=jax.ShapeDtypeStruct((half, cols + TILE), F32)
    )(own, other)
    packed = packed.astype(F16).reshape(16, mine, cols + TILE)
    packed = lax.all_to_all(packed, ("yh", "z"), 0, 0, tiled=True).astype(F32)
    basis_grad = pl.pallas_call(
        lambda *refs: unpack_kernel(math.sqrt(exposures), *refs),
        out_shape=jax.ShapeDtypeStruct((mine, cols), F32),
    )(packed)

    for axis, bit in reversed(STAGES):
        up = upper(axis, bit)
        n = coef_term.shape[0] // 2
        low, high = coef_term[:n], coef_term[n:]
        came = partner(jnp.where(up, low, high), axis, bit)
        coef_term = jnp.where(up, high, low) + came
    coef_grad = coef_term.T / math.sqrt(pixels)
    return (coef_grad, basis_grad)


def solution(mesh):
    fine = Mesh(mesh.devices.reshape(2, 8, 2, 4, 4), ("yh", "z", "c", "x", "yl"))
    exp, pix = ("yh", "z", "c"), ("x", "yl")
    placed = (
        P(exp, pix),
        P(exp, pix),
        P(exp, pix),
        P(exp, None),
        P(None, pix),
        P(exp, pix),
        P(exp, pix),
    )
    return jax.shard_map(
        body,
        mesh=fine,
        in_specs=placed,
        out_specs=(P(exp, pix), P(exp, pix)),
        check_vma=False,
    )
```

```python
import math

import jax
import jax.numpy as jnp
from jax import lax
from jax.experimental import pallas as pl
from jax.experimental.pallas import tpu as pltpu
from jax.sharding import Mesh
from jax.sharding import PartitionSpec as P

TILE = 128
BF16, F32, I16, I32 = jnp.bfloat16, jnp.float32, jnp.int16, jnp.int32
FOUR = range(4)
BASE, RUNG_BITS, LARGEST = 14, (64, 32, 16, 8, 4, 2, 1), 32767.0


def partner(value, axis, flip):
    if flip == 0:
        return value
    return lax.ppermute(value, axis, [(i, i ^ flip) for i in range(lax.axis_size(axis))])


def fused_kernel(
    trans_ref, ivar_ref, mask_ref, tangent_ref, coef_ref, coef_t_ref, full_ref, basis_ref,
    own_ref, other_ref, *coef_outs,
):
    step = pl.program_id(0)
    width = trans_ref.shape[1]
    x, y = lax.axis_index("x"), lax.axis_index("yl")
    count = basis_ref.shape[0] // 16
    basis = jnp.concatenate(
        [
            basis_ref[pl.ds(pl.multiple_of(((x ^ i) * 4 + (y ^ j)) * count, count), count), :]
            for i in FOUR
            for j in FOUR
        ],
        axis=0,
    )
    moved = lax.dot_general(
        tangent_ref[...], basis, (((0,), (0,)), ((), ())), preferred_element_type=F32
    ) + jnp.dot(coef_ref[...], full_ref[...], preferred_element_type=F32)
    lanes = lax.broadcasted_iota(I32, mask_ref.shape, 1)
    parts = []
    for t in range(width // TILE):
        part = slice(t * TILE, (t + 1) * TILE)
        here = jnp.where(lanes == step * (width // TILE) + t, mask_ref[...].astype(F32), 0.0)
        column = jnp.sum(here, axis=1, keepdims=True)
        trans = trans_ref[:, part].astype(F32)
        weights = trans * trans * ivar_ref[:, part].astype(F32) * column
        parts.append((weights * moved[:, part]).astype(BF16))
    weighted = jnp.concatenate(parts, axis=1)
    sums = jnp.dot(coef_t_ref[...], weighted, preferred_element_type=F32)
    half = own_ref.shape[0]
    own_ref[...] = sums[:half]
    other_ref[...] = sums[half:]
    term = lax.dot_general(
        basis, weighted, (((1,), (1,)), ((), ())), preferred_element_type=F32
    )
    rows = coef_outs[0].shape[0]

    @pl.when(step == 0)
    def _():
        for i, out in enumerate(coef_outs):
            out[...] = term[i * rows : (i + 1) * rows]

    @pl.when(step > 0)
    def _():
        for i, out in enumerate(coef_outs):
            out[...] += term[i * rows : (i + 1) * rows]


def pack_kernel(own_ref, other_ref, out_ref):
    total = own_ref[...] + other_ref[...]
    cols = total.shape[1]
    largest = jnp.max(jnp.abs(total), axis=1, keepdims=True) * 2.0**-BASE
    scale = jnp.full_like(largest, 2.0**-BASE)
    rung = jnp.zeros_like(largest)
    for bit in RUNG_BITS:
        fits = largest * 2.0**bit <= LARGEST
        largest = jnp.where(fits, largest * 2.0**bit, largest)
        scale = jnp.where(fits, scale * 2.0**bit, scale)
        rung = jnp.where(fits, rung + bit, rung)
    codes = jnp.round(total * scale).astype(I32).astype(I16)
    out_ref[:, :, :cols] = codes.reshape(*out_ref.shape[:2], cols)
    rungs = jnp.broadcast_to(rung, (total.shape[0], TILE)).astype(I32).astype(I16)
    out_ref[:, :, cols:] = rungs.reshape(*out_ref.shape[:2], TILE)


def unpack_kernel(divisor, in_ref, out_ref):
    cols = out_ref.shape[1]
    total = [None] * (cols // TILE)
    for i in range(in_ref.shape[0]):
        rung = in_ref[i, :, cols : cols + TILE].astype(I32)
        inverse = jnp.full(rung.shape, 2.0**BASE, F32)
        for bit in RUNG_BITS:
            inverse = inverse * jnp.where((rung & bit) != 0, F32(2.0**-bit), F32(1.0))
        for t in range(cols // TILE):
            term = in_ref[i, :, t * TILE : (t + 1) * TILE].astype(I32).astype(F32) * inverse
            total[t] = term if i == 0 else total[t] + term
    for t in range(cols // TILE):
        out_ref[:, t * TILE : (t + 1) * TILE] = total[t] * (1.0 / divisor)


def body(transmission, inverse_var, pixel_mask, coef, basis, coef_tangent, basis_tangent):
    rows, cols = transmission.shape
    rank = basis.shape[0]
    half, mine, ours = rank // 2, rank // 32, rank // 16
    exposures, pixels = rows * 32, cols * 16
    core = lax.axis_index("c")

    spread = jnp.broadcast_to(basis_tangent[None], (16, mine, cols))
    arrived = lax.all_to_all(spread, ("yh", "z"), 0, 0, tiled=True)

    tangent = coef_tangent.T
    tangent = jnp.concatenate([partner(tangent, "yl", j) for j in FOUR], axis=0)
    tangent = jnp.concatenate([partner(tangent, "x", i) for i in FOUR], axis=0)

    coef_t = coef.T.reshape(16, 2, mine, rows).transpose(1, 0, 2, 3).reshape(rank, rows)
    coef_p = coef_t.T
    coef_own = jnp.concatenate(
        [
            lax.dynamic_slice_in_dim(coef_t, core * half, half, 0),
            lax.dynamic_slice_in_dim(coef_t, (1 - core) * half, half, 0),
        ],
        axis=0,
    )

    full = lax.all_gather(arrived.reshape(half, cols), "c", axis=0, tiled=True)
    width = 256
    whole = lambda *shape: pl.BlockSpec(shape, lambda i: (0,) * len(shape))
    tall = lambda n: pl.BlockSpec((n, width), lambda i: (0, i))
    own, other, *terms = pl.pallas_call(
        fused_kernel,
        grid=(cols // width,),
        in_specs=[
            tall(rows), tall(rows), whole(rows, cols // TILE), whole(rank, rows),
            whole(rows, rank), whole(rank, rows), tall(rank), tall(rank),
        ],
        out_specs=[tall(half), tall(half)] + [whole(rank // 4, rows)] * 4,
        out_shape=[jax.ShapeDtypeStruct((half, cols), F32)] * 2
        + [jax.ShapeDtypeStruct((rank // 4, rows), F32)] * 4,
        compiler_params=pltpu.CompilerParams(vmem_limit_bytes=24 << 20),
        cost_estimate=pl.CostEstimate(
            flops=8 * rows * cols * rank, bytes_accessed=6 * rows * cols, transcendentals=0
        ),
    )(transmission, inverse_var, pixel_mask, tangent, coef_p, coef_own, full, basis)

    other = lax.ppermute(other, "c", [(0, 1), (1, 0)])
    packed = pl.pallas_call(
        pack_kernel, out_shape=jax.ShapeDtypeStruct((16, mine, cols + TILE), I16)
    )(own, other)
    packed = lax.all_to_all(packed, ("yh", "z"), 0, 0, tiled=True)
    basis_grad = pl.pallas_call(
        lambda *refs: unpack_kernel(math.sqrt(exposures), *refs),
        out_shape=jax.ShapeDtypeStruct((mine, cols), F32),
    )(packed)

    term = sum(partner(terms[i], "x", i) for i in FOUR)
    term = sum(partner(term[j * ours : (j + 1) * ours], "yl", j) for j in FOUR)
    coef_grad = term.T / math.sqrt(pixels)
    return (coef_grad, basis_grad)


def solution(mesh):
    fine = Mesh(mesh.devices.reshape(2, 8, 2, 4, 4), ("yh", "z", "c", "x", "yl"))
    exp, pix = ("yh", "z", "c"), ("x", "yl")
    placed = (
        P(exp, pix),
        P(exp, pix),
        P(exp, pix),
        P(exp, None),
        P(None, pix),
        P(exp, pix),
        P(exp, pix),
    )
    return jax.shard_map(
        body,
        mesh=fine,
        in_specs=placed,
        out_specs=(P(exp, pix), P(exp, pix)),
        check_vma=False,
    )
```

```python
import math

import jax
import jax.numpy as jnp
from jax import lax
from jax.experimental import pallas as pl
from jax.experimental.pallas import tpu as pltpu
from jax.sharding import Mesh
from jax.sharding import PartitionSpec as P

TILE = 128
BF16, F32, I16, I32 = jnp.bfloat16, jnp.float32, jnp.int16, jnp.int32
BASE, RUNG_BITS, LARGEST = 14, (64, 32, 16, 8, 4, 2, 1), 32767.0


def partner(value, axis, flip):
    return lax.ppermute(value, axis, [(i, i ^ flip) for i in range(lax.axis_size(axis))])


def first_kernel(trans_ref, ivar_ref, mask_ref, tangent_ref, basis_ref, weights_ref, moved_ref):
    step = pl.program_id(0)
    tiles = trans_ref.shape[1] // TILE
    lanes = lax.broadcasted_iota(I32, mask_ref.shape, 1)
    mask = mask_ref[...].astype(F32)
    for t in range(tiles):
        part = slice(t * TILE, (t + 1) * TILE)
        column = jnp.sum(jnp.where(lanes == step * tiles + t, mask, 0.0), axis=1, keepdims=True)
        trans = trans_ref[:, part].astype(F32)
        weights_ref[:, part] = trans * trans * ivar_ref[:, part].astype(F32) * column
    moved_ref[...] = lax.dot_general(
        tangent_ref[...], basis_ref[...], (((0,), (0,)), ((), ())), preferred_element_type=F32
    )


def second_kernel(
    weights_ref, moved_ref, coef_ref, coef_t_ref, full_ref, basis_ref,
    own_ref, other_ref, kept_ref, given_ref,
):
    moved = moved_ref[...] + jnp.dot(coef_ref[...], full_ref[...], preferred_element_type=F32)
    weighted = (weights_ref[...] * moved).astype(BF16)
    half = own_ref.shape[0]
    core = lax.axis_index("c")
    for out, which in ((own_ref, core), (other_ref, 1 - core)):
        rows = pl.ds(pl.multiple_of(which * half, half), half)
        out[...] = jnp.dot(coef_t_ref[rows, :], weighted, preferred_element_type=F32)
    x, y = lax.axis_index("x"), lax.axis_index("yl")
    count = basis_ref.shape[0] // 16
    for out, a in ((kept_ref, 0), (given_ref, 1)):
        basis = jnp.concatenate(
            [
                basis_ref[
                    pl.ds(pl.multiple_of(((x ^ (a + 2 * c)) * 4 + (y ^ (b + 2 * d))) * count, count), count), :
                ]
                for b in (0, 1)
                for c in (0, 1)
                for d in (0, 1)
            ],
            axis=0,
        )
        term = lax.dot_general(
            basis, weighted, (((1,), (1,)), ((), ())), preferred_element_type=F32
        )

        @pl.when(pl.program_id(0) == 0)
        def _():
            out[...] = term

        @pl.when(pl.program_id(0) > 0)
        def _():
            out[...] += term


def pack_kernel(own_ref, other_ref, out_ref):
    total = own_ref[...] + other_ref[...]
    cols = total.shape[1]
    largest = jnp.max(jnp.abs(total), axis=1, keepdims=True) * 2.0**-BASE
    scale = jnp.full_like(largest, 2.0**-BASE)
    rung = jnp.zeros_like(largest)
    for bit in RUNG_BITS:
        fits = largest * 2.0**bit <= LARGEST
        largest = jnp.where(fits, largest * 2.0**bit, largest)
        scale = jnp.where(fits, scale * 2.0**bit, scale)
        rung = jnp.where(fits, rung + bit, rung)
    codes = jnp.round(total * scale).astype(I32).astype(I16)
    out_ref[:, :, :cols] = codes.reshape(*out_ref.shape[:2], cols)
    rungs = jnp.broadcast_to(rung, (total.shape[0], TILE)).astype(I32).astype(I16)
    out_ref[:, :, cols:] = rungs.reshape(*out_ref.shape[:2], TILE)


def unpack_kernel(in_ref, own_ref, other_ref):
    count, cols = own_ref.shape
    first = lax.axis_index("yh") == 0
    total = [None] * (cols // TILE)
    for i in range(in_ref.shape[0]):
        rung = in_ref[i, :, cols : cols + TILE].astype(I32)
        inverse = jnp.full(rung.shape, 2.0**BASE, F32)
        for bit in RUNG_BITS:
            inverse = inverse * jnp.where((rung & bit) != 0, F32(2.0**-bit), F32(1.0))
        for t in range(cols // TILE):
            term = in_ref[i, :, t * TILE : (t + 1) * TILE].astype(I32).astype(F32) * inverse
            total[t] = term if i == 0 else total[t] + term
    for t in range(cols // TILE):
        part = slice(t * TILE, (t + 1) * TILE)
        low, high = total[t][:count], total[t][count:]
        own_ref[:, part] = jnp.where(first, low, high)
        other_ref[:, part] = jnp.where(first, high, low)


def body(transmission, inverse_var, pixel_mask, coef, basis, coef_tangent, basis_tangent):
    rows, cols = transmission.shape
    rank = basis.shape[0]
    half, mine, ours = rank // 2, rank // 32, rank // 16
    exposures, pixels = rows * 32, cols * 16

    across = partner(basis_tangent, "yh", 1)
    tangent = jnp.broadcast_to(coef_tangent.T[None], (16, ours, rows))
    tangent = lax.all_to_all(tangent, ("x", "yl"), 0, 0, tiled=True).reshape(rank, rows)
    across, tangent = lax.optimization_barrier((across, tangent))

    first = lax.axis_index("yh") == 0
    pair = jnp.stack(
        [jnp.where(first, basis_tangent, across), jnp.where(first, across, basis_tangent)]
    ).reshape(1, 2 * mine, cols)
    arrived = lax.all_to_all(jnp.broadcast_to(pair, (8, 2 * mine, cols)), "z", 0, 0, tiled=True)
    full = lax.all_gather(arrived.reshape(half, cols), "c", axis=0, tiled=True)
    coef_t = coef.T.reshape(2, 8, 2, mine, rows).transpose(2, 1, 0, 3, 4).reshape(rank, rows)
    coef_p = coef_t.T

    width = 256
    whole = lambda *shape: pl.BlockSpec(shape, lambda i: (0,) * len(shape))
    tall = lambda n: pl.BlockSpec((n, width), lambda i: (0, i))
    params = pltpu.CompilerParams(vmem_limit_bytes=24 << 20)
    weights, moved = pl.pallas_call(
        first_kernel,
        grid=(cols // width,),
        in_specs=[tall(rows), tall(rows), whole(rows, cols // TILE), whole(rank, rows), tall(rank)],
        out_specs=[tall(rows), tall(rows)],
        out_shape=[pltpu.HBM((rows, cols), F32)] * 2,
        compiler_params=params,
        cost_estimate=pl.CostEstimate(
            flops=2 * rows * cols * rank, bytes_accessed=12 * rows * cols, transcendentals=0
        ),
    )(transmission, inverse_var, pixel_mask, tangent, basis)
    own, other, kept, given = pl.pallas_call(
        second_kernel,
        grid=(cols // width,),
        in_specs=[
            tall(rows), tall(rows), whole(rows, rank), whole(rank, rows), tall(rank), tall(rank),
        ],
        out_specs=[tall(half), tall(half), whole(half, rows), whole(half, rows)],
        out_shape=[jax.ShapeDtypeStruct((half, cols), F32)] * 2
        + [jax.ShapeDtypeStruct((half, rows), F32)] * 2,
        compiler_params=params,
        cost_estimate=pl.CostEstimate(
            flops=6 * rows * cols * rank, bytes_accessed=8 * rows * cols, transcendentals=0
        ),
    )(weights, moved, coef_p, coef_t, full, basis)

    small = pltpu.CompilerParams(vmem_limit_bytes=8 << 20)
    other = partner(other, "c", 1)
    packed = pl.pallas_call(
        pack_kernel,
        out_shape=jax.ShapeDtypeStruct((8, 2 * mine, cols + TILE), I16),
        compiler_params=small,
    )(own, other)
    packed = lax.all_to_all(packed, "z", 0, 0, tiled=True)
    own, other = pl.pallas_call(
        unpack_kernel,
        out_shape=[jax.ShapeDtypeStruct((mine, cols), F32)] * 2,
        compiler_params=small,
    )(packed)
    basis_grad = (own + partner(other, "yh", 1)) * (1.0 / math.sqrt(exposures))

    for axis, flip in (("x", 1), ("yl", 1), ("x", 2), ("yl", 2)):
        total = kept + partner(given, axis, flip)
        n = total.shape[0] // 2
        kept, given = total[:n], total[n:]
    coef_grad = total.T / math.sqrt(pixels)
    return (coef_grad, basis_grad)


def solution(mesh):
    fine = Mesh(mesh.devices.reshape(2, 8, 2, 4, 4), ("yh", "z", "c", "x", "yl"))
    exp, pix = ("yh", "z", "c"), ("x", "yl")
    placed = (
        P(exp, pix),
        P(exp, pix),
        P(exp, pix),
        P(exp, None),
        P(None, pix),
        P(exp, pix),
        P(exp, pix),
    )
    return jax.shard_map(
        body,
        mesh=fine,
        in_specs=placed,
        out_specs=(P(exp, pix), P(exp, pix)),
        check_vma=False,
    )
```

```python
import functools
import math

import jax
import jax.numpy as jnp
from jax import lax
from jax.experimental import pallas as pl
from jax.experimental.pallas import tpu as pltpu
from jax.sharding import Mesh
from jax.sharding import PartitionSpec as P

TILE = 128
BF16, F32, I16, I32 = jnp.bfloat16, jnp.float32, jnp.int16, jnp.int32
BASE, RUNG_BITS, LARGEST = 14, (64, 32, 16, 8, 4, 2, 1), 32767.0


def partner(value, axis, flip):
    return lax.ppermute(value, axis, [(i, i ^ flip) for i in range(lax.axis_size(axis))])


def in_hbm(value):
    return pltpu.with_memory_space_constraint(value, pltpu.HBM)


def block_of(ref, which, count):
    return ref[pl.ds(pl.multiple_of(which * count, count), count), :]


def fused_kernel(
    trans_ref, ivar_ref, mask_ref, tangent_ref, coef_t_ref, full_ref, basis_ref,
    own_ref, other_ref, kept_ref, given_ref,
):
    step = pl.program_id(0)
    tiles = trans_ref.shape[1] // TILE
    moved = lax.dot_general(
        tangent_ref[...], basis_ref[...], (((0,), (0,)), ((), ())), preferred_element_type=F32
    ) + lax.dot_general(
        coef_t_ref[...], full_ref[...], (((0,), (0,)), ((), ())), preferred_element_type=F32
    )
    mask = mask_ref[...].astype(F32).T
    lanes = lax.broadcasted_iota(I32, mask.shape, 1)
    parts = []
    for t in range(tiles):
        part = slice(t * TILE, (t + 1) * TILE)
        column = jnp.sum(jnp.where(lanes == step * tiles + t, mask, 0.0), axis=1, keepdims=True)
        trans = trans_ref[:, part].astype(F32)
        weights = trans * trans * ivar_ref[:, part].astype(F32) * column
        parts.append((weights * moved[:, part]).astype(BF16))
    weighted = jnp.concatenate(parts, axis=1)

    count = basis_ref.shape[0] // 16
    core, z = lax.axis_index("c"), lax.axis_index("z")
    for out, which in ((own_ref, core), (other_ref, 1 - core)):
        rows = [
            block_of(coef_t_ref, which * 8 + (z ^ (a + 2 * b + 4 * c)), count)
            for a in (0, 1)
            for b in (0, 1)
            for c in (0, 1)
        ]
        out[...] = jnp.dot(jnp.concatenate(rows, axis=0), weighted, preferred_element_type=F32)
    x, y = lax.axis_index("x"), lax.axis_index("yl")
    for out, a in ((kept_ref, 0), (given_ref, 1)):
        rows = [
            block_of(basis_ref, (x ^ (a + 2 * c)) * 4 + (y ^ (b + 2 * d)), count)
            for b in (0, 1)
            for c in (0, 1)
            for d in (0, 1)
        ]
        term = lax.dot_general(
            jnp.concatenate(rows, axis=0), weighted, (((1,), (1,)), ((), ())),
            preferred_element_type=F32,
        )

        @pl.when(step == 0)
        def _():
            out[...] = term

        @pl.when(step > 0)
        def _():
            out[...] += term


def encode(total, out_ref):
    cols = total.shape[1]
    largest = jnp.max(jnp.abs(total), axis=1, keepdims=True) * 2.0**-BASE
    scale = jnp.full_like(largest, 2.0**-BASE)
    rung = jnp.zeros_like(largest)
    for bit in RUNG_BITS:
        fits = largest * 2.0**bit <= LARGEST
        largest = jnp.where(fits, largest * 2.0**bit, largest)
        scale = jnp.where(fits, scale * 2.0**bit, scale)
        rung = jnp.where(fits, rung + bit, rung)
    out_ref[:, :cols] = jnp.round(total * scale).astype(I32).astype(I16)
    rungs = jnp.broadcast_to(rung, (total.shape[0], TILE))
    out_ref[:, cols:] = rungs.astype(I32).astype(I16)


def decode(code_ref):
    cols = code_ref.shape[1] - TILE
    rung = code_ref[:, cols:].astype(I32)
    inverse = jnp.full(rung.shape, 2.0**BASE, F32)
    for bit in RUNG_BITS:
        inverse = inverse * jnp.where((rung & bit) != 0, F32(2.0**-bit), F32(1.0))
    return jnp.concatenate(
        [
            code_ref[:, t * TILE : (t + 1) * TILE].astype(I32).astype(F32) * inverse
            for t in range(cols // TILE)
        ],
        axis=1,
    )


def halve_kernel(coded, by_y, mine_ref, came_ref, keep_ref, give_ref):
    total = mine_ref[...] + (decode(came_ref) if coded else came_ref[...])
    n = keep_ref.shape[0]
    keep, give = total[:n], total[n:]
    if by_y:
        first = lax.axis_index("yh") == 0
        keep, give = jnp.where(first, keep, give), jnp.where(first, give, keep)
    keep_ref[...] = keep
    encode(give, give_ref)


def last_kernel(divisor, mine_ref, came_ref, out_ref):
    out_ref[...] = (mine_ref[...] + decode(came_ref)) * (1.0 / divisor)


def body(transmission, inverse_var, pixel_mask, coef, basis, coef_tangent, basis_tangent):
    rows, cols = transmission.shape
    rank = basis.shape[0]
    half, mine, ours = rank // 2, rank // 32, rank // 16
    exposures, pixels = rows * 32, cols * 16

    across = partner(basis_tangent, "yh", 1)
    tangent = jnp.broadcast_to(coef_tangent.T[None], (16, ours, rows))
    tangent = lax.all_to_all(tangent, ("x", "yl"), 0, 0, tiled=True).reshape(rank, rows)
    coef_t = coef.T.reshape(2, 8, 2, mine, rows).transpose(2, 1, 0, 3, 4).reshape(rank, rows)
    across, tangent, coef_t = lax.optimization_barrier((across, tangent, coef_t))

    first = lax.axis_index("yh") == 0
    pair = jnp.stack(
        [jnp.where(first, basis_tangent, across), jnp.where(first, across, basis_tangent)]
    ).reshape(1, 2 * mine, cols)
    arrived = lax.all_to_all(jnp.broadcast_to(pair, (8, 2 * mine, cols)), "z", 0, 0, tiled=True)
    full = lax.all_gather(arrived.reshape(half, cols), "c", axis=0, tiled=True)

    width = cols // 2
    whole = lambda *shape: pl.BlockSpec(shape, lambda i: (0,) * len(shape))
    tall = lambda n: pl.BlockSpec((n, width), lambda i: (0, i))
    own, other, kept, given = pl.pallas_call(
        fused_kernel,
        grid=(cols // width,),
        in_specs=[
            tall(rows), tall(rows), whole(cols // TILE, rows), whole(rank, rows),
            whole(rank, rows), tall(rank), tall(rank),
        ],
        out_specs=[tall(half), tall(half), whole(half, rows), whole(half, rows)],
        out_shape=[jax.ShapeDtypeStruct((half, cols), F32)] * 2
        + [jax.ShapeDtypeStruct((half, rows), F32)] * 2,
        compiler_params=pltpu.CompilerParams(vmem_limit_bytes=32 << 20),
        cost_estimate=pl.CostEstimate(
            flops=8 * rows * cols * rank, bytes_accessed=6 * rows * cols, transcendentals=0
        ),
    )(*map(in_hbm, (transmission, inverse_var)), pixel_mask.T, tangent, coef_t, full, basis)

    small = pltpu.CompilerParams(vmem_limit_bytes=8 << 20)
    came = partner(other, "c", 1)
    for coded, (axis, flip) in enumerate((("z", 1), ("z", 2), ("z", 4), ("yh", 1))):
        n = own.shape[0] // 2
        own, give = pl.pallas_call(
            functools.partial(halve_kernel, coded > 0, axis == "yh"),
            out_shape=[
                jax.ShapeDtypeStruct((n, cols), F32),
                jax.ShapeDtypeStruct((n, cols + TILE), I16),
            ],
            compiler_params=small,
        )(own, came)
        came = partner(give, axis, flip)
    basis_grad = pl.pallas_call(
        functools.partial(last_kernel, math.sqrt(exposures)),
        out_shape=jax.ShapeDtypeStruct((mine, cols), F32),
        compiler_params=small,
    )(own, came)

    for axis, flip in (("x", 1), ("yl", 1), ("x", 2), ("yl", 2)):
        total = kept + partner(given, axis, flip)
        n = total.shape[0] // 2
        kept, given = total[:n], total[n:]
    coef_grad = total.T / math.sqrt(pixels)
    return (coef_grad, basis_grad)


def solution(mesh):
    fine = Mesh(mesh.devices.reshape(2, 8, 2, 4, 4), ("yh", "z", "c", "x", "yl"))
    exp, pix = ("yh", "z", "c"), ("x", "yl")
    placed = (
        P(exp, pix),
        P(exp, pix),
        P(exp, pix),
        P(exp, None),
        P(None, pix),
        P(exp, pix),
        P(exp, pix),
    )
    return jax.shard_map(
        body,
        mesh=fine,
        in_specs=placed,
        out_specs=(P(exp, pix), P(exp, pix)),
        check_vma=False,
    )
```

```python
import functools
import math

import jax
import jax.numpy as jnp
from jax import lax
from jax.experimental import pallas as pl
from jax.experimental.pallas import tpu as pltpu
from jax.sharding import Mesh
from jax.sharding import PartitionSpec as P

TILE = 128
BF16, F32, I16, I32 = jnp.bfloat16, jnp.float32, jnp.int16, jnp.int32
BASE, RUNG_BITS, LARGEST = 14, (64, 32, 16, 8, 4, 2, 1), 32767.0


def partner(value, axis, flip):
    return lax.ppermute(value, axis, [(i, i ^ flip) for i in range(lax.axis_size(axis))])


def in_hbm(value):
    return pltpu.with_memory_space_constraint(value, pltpu.HBM)


def block_of(ref, which, count):
    return ref[pl.ds(pl.multiple_of(which * count, count), count), :]


def fused_kernel(
    trans_ref, ivar_ref, mask_ref, tangent_ref, coef_t_ref, full_ref, basis_ref,
    own_ref, other_ref, coef_ref,
):
    step = pl.program_id(0)
    tiles = trans_ref.shape[1] // TILE
    moved = lax.dot_general(
        tangent_ref[...], basis_ref[...], (((0,), (0,)), ((), ())), preferred_element_type=F32
    ) + lax.dot_general(
        coef_t_ref[...], full_ref[...], (((0,), (0,)), ((), ())), preferred_element_type=F32
    )
    mask = mask_ref[...].astype(F32).T
    lanes = lax.broadcasted_iota(I32, mask.shape, 1)
    parts = []
    for t in range(tiles):
        part = slice(t * TILE, (t + 1) * TILE)
        column = jnp.sum(jnp.where(lanes == step * tiles + t, mask, 0.0), axis=1, keepdims=True)
        trans = trans_ref[:, part].astype(F32)
        weights = trans * trans * ivar_ref[:, part].astype(F32) * column
        parts.append((weights * moved[:, part]).astype(BF16))
    weighted = jnp.concatenate(parts, axis=1)

    half = own_ref.shape[0]
    core = lax.axis_index("c")
    for out, which in ((own_ref, core), (other_ref, 1 - core)):
        rows = block_of(coef_t_ref, which, half)
        out[...] = jnp.dot(rows, weighted, preferred_element_type=F32)
    term = lax.dot_general(
        basis_ref[...], weighted, (((1,), (1,)), ((), ())), preferred_element_type=F32
    )

    @pl.when(step == 0)
    def _():
        coef_ref[...] = term

    @pl.when(step > 0)
    def _():
        coef_ref[...] += term


def encode(total, out_ref):
    cols = total.shape[1]
    largest = jnp.max(jnp.abs(total), axis=1, keepdims=True) * 2.0**-BASE
    scale = jnp.full_like(largest, 2.0**-BASE)
    rung = jnp.zeros_like(largest)
    for bit in RUNG_BITS:
        fits = largest * 2.0**bit <= LARGEST
        largest = jnp.where(fits, largest * 2.0**bit, largest)
        scale = jnp.where(fits, scale * 2.0**bit, scale)
        rung = jnp.where(fits, rung + bit, rung)
    out_ref[:, :cols] = jnp.round(total * scale).astype(I32).astype(I16)
    rungs = jnp.broadcast_to(rung, (total.shape[0], TILE))
    out_ref[:, cols:] = rungs.astype(I32).astype(I16)


def decode(code_ref):
    cols = code_ref.shape[1] - TILE
    rung = code_ref[:, cols:].astype(I32)
    inverse = jnp.full(rung.shape, 2.0**BASE, F32)
    for bit in RUNG_BITS:
        inverse = inverse * jnp.where((rung & bit) != 0, F32(2.0**-bit), F32(1.0))
    return jnp.concatenate(
        [
            code_ref[:, t * TILE : (t + 1) * TILE].astype(I32).astype(F32) * inverse
            for t in range(cols // TILE)
        ],
        axis=1,
    )


def pack_kernel(*refs):
    *terms, out_ref = refs
    encode(sum(term[...] for term in terms), out_ref)


def part_of(ref, i, count):
    return ref.at[i * count : (i + 1) * count]


def halve_kernel(in_ref, keep_ref, give_ref):
    n = keep_ref.shape[0]
    total = sum(decode(part_of(in_ref, i, 2 * n)) for i in range(in_ref.shape[0] // (2 * n)))
    first = lax.axis_index("yh") == 0
    low, high = total[:n], total[n:]
    keep_ref[...] = jnp.where(first, low, high)
    encode(jnp.where(first, high, low), give_ref)


def last_kernel(divisor, mine_ref, came_ref, out_ref):
    out_ref[...] = (mine_ref[...] + decode(came_ref)) * (1.0 / divisor)


def coef_kernel(divisor, in_ref, out_ref):
    n = out_ref.shape[0]
    total = sum(decode(part_of(in_ref, i, n)) for i in range(in_ref.shape[0] // n))
    out_ref[...] = total * (1.0 / divisor)


def body(transmission, inverse_var, pixel_mask, coef, basis, coef_tangent, basis_tangent):
    rows, cols = transmission.shape
    rank = basis.shape[0]
    half, mine, ours = rank // 2, rank // 32, rank // 16
    exposures, pixels = rows * 32, cols * 16

    across = partner(basis_tangent, "yh", 1)
    coef_t = coef.T.reshape(2, 8, 2, mine, rows).transpose(2, 1, 0, 3, 4).reshape(rank, rows)
    tangent = jnp.broadcast_to(coef_tangent.T[None], (16, ours, rows))
    across, coef_t, tangent = lax.optimization_barrier((across, coef_t, tangent))
    tangent = lax.all_to_all(tangent, ("x", "yl"), 0, 0, tiled=True).reshape(rank, rows)
    across, tangent = lax.optimization_barrier((across, tangent))

    first = lax.axis_index("yh") == 0
    pair = jnp.stack(
        [jnp.where(first, basis_tangent, across), jnp.where(first, across, basis_tangent)]
    ).reshape(1, 2 * mine, cols)
    arrived = lax.all_to_all(jnp.broadcast_to(pair, (8, 2 * mine, cols)), "z", 0, 0, tiled=True)
    full = lax.all_gather(arrived.reshape(half, cols), "c", axis=0, tiled=True)

    width = cols // 2
    whole = lambda *shape: pl.BlockSpec(shape, lambda i: (0,) * len(shape))
    tall = lambda n: pl.BlockSpec((n, width), lambda i: (0, i))
    own, other, coef_term = pl.pallas_call(
        fused_kernel,
        grid=(cols // width,),
        in_specs=[
            tall(rows), tall(rows), whole(cols // TILE, rows), whole(rank, rows),
            whole(rank, rows), tall(rank), tall(rank),
        ],
        out_specs=[tall(half), tall(half), whole(rank, rows)],
        out_shape=[
            jax.ShapeDtypeStruct((half, cols), F32),
            jax.ShapeDtypeStruct((half, cols), F32),
            jax.ShapeDtypeStruct((rank, rows), F32),
        ],
        compiler_params=pltpu.CompilerParams(vmem_limit_bytes=32 << 20),
        cost_estimate=pl.CostEstimate(
            flops=8 * rows * cols * rank, bytes_accessed=6 * rows * cols, transcendentals=0
        ),
    )(*map(in_hbm, (transmission, inverse_var)), pixel_mask.T, tangent, coef_t, full, basis)

    small = lambda kernel, *shapes: pl.pallas_call(
        kernel,
        out_shape=[jax.ShapeDtypeStruct(*shape) for shape in shapes],
        compiler_params=pltpu.CompilerParams(vmem_limit_bytes=8 << 20),
    )
    exchange = lambda value, axis, n: lax.all_to_all(
        value.reshape(n, -1, value.shape[1]), axis, 0, 0, tiled=True
    ).reshape(value.shape)

    came = partner(other, "c", 1)
    [codes] = small(pack_kernel, ((rank, rows + TILE), I16))(coef_term)
    codes = exchange(codes, ("x", "yl"), 16)
    [coef_grad] = small(
        functools.partial(coef_kernel, math.sqrt(pixels)), ((ours, rows), F32)
    )(codes)

    [codes] = small(pack_kernel, ((half, cols + TILE), I16))(own, came)
    codes = exchange(codes, "z", 8)
    keep, give = small(halve_kernel, ((mine, cols), F32), ((mine, cols + TILE), I16))(codes)
    [basis_grad] = small(
        functools.partial(last_kernel, math.sqrt(exposures)), ((mine, cols), F32)
    )(keep, partner(give, "yh", 1))
    return (coef_grad.T, basis_grad)


def solution(mesh):
    fine = Mesh(mesh.devices.reshape(2, 8, 2, 4, 4), ("yh", "z", "c", "x", "yl"))
    exp, pix = ("yh", "z", "c"), ("x", "yl")
    placed = (
        P(exp, pix),
        P(exp, pix),
        P(exp, pix),
        P(exp, None),
        P(None, pix),
        P(exp, pix),
        P(exp, pix),
    )
    return jax.shard_map(
        body,
        mesh=fine,
        in_specs=placed,
        out_specs=(P(exp, pix), P(exp, pix)),
        check_vma=False,
    )
```

```python
import functools
import math

import jax
import jax.numpy as jnp
from jax import lax
from jax.experimental import pallas as pl
from jax.experimental.pallas import tpu as pltpu
from jax.sharding import Mesh
from jax.sharding import PartitionSpec as P

TILE = 128
BF16, F32, I16, I32 = jnp.bfloat16, jnp.float32, jnp.int16, jnp.int32
BASE, RUNG_BITS, LARGEST = 14, (64, 32, 16, 8, 4, 2, 1), 32767.0


def partner(value, axis, flip):
    return lax.ppermute(value, axis, [(i, i ^ flip) for i in range(lax.axis_size(axis))])


def in_hbm(value):
    return pltpu.with_memory_space_constraint(value, pltpu.HBM)


def block_of(ref, which, count):
    return ref[pl.ds(pl.multiple_of(which * count, count), count), :]


def fused_kernel(
    trans_ref, ivar_ref, mask_ref, tangent_ref, coef_ref, full_ref, basis_ref,
    own_ref, other_ref, term_ref, coef_p_ref, coef_t_ref,
):
    step = pl.program_id(0)

    @pl.when(step == 0)
    def _():
        rank = coef_ref.shape[1]
        take = lax.broadcasted_iota(I32, (rank, rank), 0)
        place = lax.broadcasted_iota(I32, (rank, rank), 1)
        low, mid, high = place & 7, place & 112, ((place >> 3) & 1) * 128 + ((place >> 7) & 1) * 8
        chosen = (take == low + mid + high).astype(BF16)
        coef = coef_ref[...]
        coef_p_ref[...] = jnp.dot(coef, chosen, preferred_element_type=F32).astype(BF16)
        coef_t_ref[...] = lax.dot_general(
            chosen, coef, (((0,), (1,)), ((), ())), preferred_element_type=F32
        ).astype(BF16)

    tiles = trans_ref.shape[1] // TILE
    moved = lax.dot_general(
        tangent_ref[...], basis_ref[...], (((0,), (0,)), ((), ())), preferred_element_type=F32
    ) + jnp.dot(coef_p_ref[...], full_ref[...], preferred_element_type=F32)
    mask = mask_ref[...].astype(F32).T
    lanes = lax.broadcasted_iota(I32, mask.shape, 1)
    parts = []
    for t in range(tiles):
        part = slice(t * TILE, (t + 1) * TILE)
        column = jnp.sum(jnp.where(lanes == step * tiles + t, mask, 0.0), axis=1, keepdims=True)
        trans = trans_ref[:, part].astype(F32)
        weights = trans * trans * ivar_ref[:, part].astype(F32) * column
        parts.append((weights * moved[:, part]).astype(BF16))
    weighted = jnp.concatenate(parts, axis=1)

    half = own_ref.shape[0]
    core = lax.axis_index("c")
    for out, which in ((own_ref, core), (other_ref, 1 - core)):
        rows = block_of(coef_t_ref, which, half)
        out[...] = jnp.dot(rows, weighted, preferred_element_type=F32)
    term = lax.dot_general(
        basis_ref[...], weighted, (((1,), (1,)), ((), ())), preferred_element_type=F32
    )

    @pl.when(step == 0)
    def _():
        term_ref[...] = term

    @pl.when(step > 0)
    def _():
        term_ref[...] += term


def encode(total, out_ref):
    cols = total.shape[1]
    largest = jnp.max(jnp.abs(total), axis=1, keepdims=True) * 2.0**-BASE
    scale = jnp.full_like(largest, 2.0**-BASE)
    rung = jnp.zeros_like(largest)
    for bit in RUNG_BITS:
        fits = largest * 2.0**bit <= LARGEST
        largest = jnp.where(fits, largest * 2.0**bit, largest)
        scale = jnp.where(fits, scale * 2.0**bit, scale)
        rung = jnp.where(fits, rung + bit, rung)
    out_ref[:, :cols] = jnp.round(total * scale).astype(I32).astype(I16)
    rungs = jnp.broadcast_to(rung, (total.shape[0], TILE))
    out_ref[:, cols:] = rungs.astype(I32).astype(I16)


def decode(code_ref):
    cols = code_ref.shape[1] - TILE
    rung = code_ref[:, cols:].astype(I32)
    inverse = jnp.full(rung.shape, 2.0**BASE, F32)
    for bit in RUNG_BITS:
        inverse = inverse * jnp.where((rung & bit) != 0, F32(2.0**-bit), F32(1.0))
    return jnp.concatenate(
        [
            code_ref[:, t * TILE : (t + 1) * TILE].astype(I32).astype(F32) * inverse
            for t in range(cols // TILE)
        ],
        axis=1,
    )


def spread_kernel(in_ref, out_ref):
    for i in range(out_ref.shape[0]):
        out_ref[i] = in_ref[...]


def spread_pair_kernel(mine_ref, other_ref, out_ref):
    mine, other = mine_ref[...].astype(F32), other_ref[...].astype(F32)
    first = lax.axis_index("yh") == 0
    pair = [jnp.where(first, mine, other), jnp.where(first, other, mine)]
    pair = jnp.concatenate(pair, axis=0).astype(BF16)
    for i in range(out_ref.shape[0]):
        out_ref[i] = pair


def pack_kernel(term_ref, out_ref):
    encode(term_ref[...], out_ref)


def add_kernel(own_ref, both_ref, out_ref):
    n = own_ref.shape[0]
    came = pl.ds(pl.multiple_of((1 - lax.axis_index("c")) * n, n), n)
    encode(own_ref[...] + decode(both_ref.at[came]), out_ref)


def part_of(ref, i, count):
    return ref.at[i * count : (i + 1) * count]


def halve_kernel(in_ref, keep_ref, give_ref):
    n = keep_ref.shape[0]
    total = sum(decode(part_of(in_ref, i, 2 * n)) for i in range(in_ref.shape[0] // (2 * n)))
    first = lax.axis_index("yh") == 0
    low, high = total[:n], total[n:]
    keep_ref[...] = jnp.where(first, low, high)
    encode(jnp.where(first, high, low), give_ref)


def last_kernel(divisor, mine_ref, came_ref, out_ref):
    out_ref[...] = (mine_ref[...] + decode(came_ref)) * (1.0 / divisor)


def coef_kernel(divisor, in_ref, out_ref):
    n = out_ref.shape[0]
    total = sum(decode(part_of(in_ref, i, n)) for i in range(in_ref.shape[0] // n))
    out_ref[...] = total * (1.0 / divisor)


def body(transmission, inverse_var, pixel_mask, coef, basis, coef_tangent, basis_tangent):
    rows, cols = transmission.shape
    rank = basis.shape[0]
    half, mine, ours = rank // 2, rank // 32, rank // 16
    exposures, pixels = rows * 32, cols * 16

    small = lambda kernel, *shapes: pl.pallas_call(
        kernel,
        out_shape=[jax.ShapeDtypeStruct(*shape) for shape in shapes],
        compiler_params=pltpu.CompilerParams(vmem_limit_bytes=8 << 20),
    )
    exchange = lambda value, axis: lax.all_to_all(value, axis, 0, 0, tiled=True)

    across = partner(basis_tangent, "yh", 1)
    [tangent] = small(spread_kernel, ((16, ours, rows), BF16))(coef_tangent.T)
    tangent = exchange(tangent, ("x", "yl")).reshape(rank, rows)
    across, tangent = lax.optimization_barrier((across, tangent))

    [pair] = small(spread_pair_kernel, ((8, 2 * mine, cols), BF16))(basis_tangent, across)
    arrived = exchange(pair, "z").reshape(half, cols)
    full = lax.all_gather(arrived, "c", axis=0, tiled=True)

    width = cols // 2
    whole = lambda *shape: pl.BlockSpec(shape, lambda i: (0,) * len(shape))
    tall = lambda n: pl.BlockSpec((n, width), lambda i: (0, i))
    own, other, term = pl.pallas_call(
        fused_kernel,
        grid=(cols // width,),
        in_specs=[
            tall(rows), tall(rows), whole(cols // TILE, rows), whole(rank, rows),
            whole(rows, rank), tall(rank), tall(rank),
        ],
        out_specs=[tall(half), tall(half), whole(rank, rows)],
        out_shape=[
            jax.ShapeDtypeStruct((half, cols), F32),
            jax.ShapeDtypeStruct((half, cols), F32),
            jax.ShapeDtypeStruct((rank, rows), F32),
        ],
        scratch_shapes=[pltpu.VMEM((rows, rank), BF16), pltpu.VMEM((rank, rows), BF16)],
        compiler_params=pltpu.CompilerParams(vmem_limit_bytes=32 << 20),
        cost_estimate=pl.CostEstimate(
            flops=8 * rows * cols * rank, bytes_accessed=6 * rows * cols, transcendentals=0
        ),
    )(*map(in_hbm, (transmission, inverse_var)), pixel_mask.T, tangent, coef, full, basis)

    [codes] = small(pack_kernel, ((half, cols + TILE), I16))(other)
    codes = lax.all_gather(codes, "c", axis=0, tiled=True)
    [codes] = small(add_kernel, ((half, cols + TILE), I16))(own, codes)
    [terms] = small(pack_kernel, ((rank, rows + TILE), I16))(term)
    codes, terms = lax.optimization_barrier((codes, terms))
    codes = exchange(codes.reshape(8, 2 * mine, cols + TILE), "z").reshape(half, cols + TILE)

    keep, give = small(halve_kernel, ((mine, cols), F32), ((mine, cols + TILE), I16))(codes)
    [basis_grad] = small(
        functools.partial(last_kernel, math.sqrt(exposures)), ((mine, cols), F32)
    )(keep, partner(give, "yh", 1))
    terms = exchange(terms.reshape(16, ours, rows + TILE), ("x", "yl")).reshape(rank, rows + TILE)
    [coef_grad] = small(
        functools.partial(coef_kernel, math.sqrt(pixels)), ((ours, rows), F32)
    )(terms)
    return (coef_grad.T, basis_grad)


def solution(mesh):
    fine = Mesh(mesh.devices.reshape(2, 8, 2, 4, 4), ("yh", "z", "c", "x", "yl"))
    exp, pix = ("yh", "z", "c"), ("x", "yl")
    placed = (
        P(exp, pix),
        P(exp, pix),
        P(exp, pix),
        P(exp, None),
        P(None, pix),
        P(exp, pix),
        P(exp, pix),
    )
    return jax.shard_map(
        body,
        mesh=fine,
        in_specs=placed,
        out_specs=(P(exp, pix), P(exp, pix)),
        check_vma=False,
    )
```

```python
import functools
import math

import jax
import jax.numpy as jnp
from jax import lax
from jax.experimental import pallas as pl
from jax.experimental.pallas import tpu as pltpu
from jax.sharding import Mesh
from jax.sharding import PartitionSpec as P

TILE = 128
BF16, F32, I16, I32 = jnp.bfloat16, jnp.float32, jnp.int16, jnp.int32
BASE, RUNG_BITS, LARGEST = 14, (64, 32, 16, 8, 4, 2, 1), 32767.0


def partner(value, axis, flip):
    return lax.ppermute(value, axis, [(i, i ^ flip) for i in range(lax.axis_size(axis))])


def in_hbm(value):
    return pltpu.with_memory_space_constraint(value, pltpu.HBM)


def block_of(ref, which, count):
    return ref[pl.ds(pl.multiple_of(which * count, count), count), :]


def fused_kernel(
    trans_ref, ivar_ref, mask_ref, tangent_ref, coef_ref, full_ref, basis_ref,
    own_ref, other_codes_ref, term_codes_ref, coef_p_ref, coef_t_ref, other_ref, term_ref,
):
    step = pl.program_id(0)

    @pl.when(step == 0)
    def _():
        rank = coef_ref.shape[1]
        take = lax.broadcasted_iota(I32, (rank, rank), 0)
        place = lax.broadcasted_iota(I32, (rank, rank), 1)
        low, mid, high = place & 7, place & 112, ((place >> 3) & 1) * 128 + ((place >> 7) & 1) * 8
        chosen = (take == low + mid + high).astype(BF16)
        coef = coef_ref[...]
        coef_p_ref[...] = jnp.dot(coef, chosen, preferred_element_type=F32).astype(BF16)
        coef_t_ref[...] = lax.dot_general(
            chosen, coef, (((0,), (1,)), ((), ())), preferred_element_type=F32
        ).astype(BF16)

    tiles = trans_ref.shape[1] // TILE
    moved = lax.dot_general(
        tangent_ref[...], basis_ref[...], (((0,), (0,)), ((), ())), preferred_element_type=F32
    ) + jnp.dot(coef_p_ref[...], full_ref[...], preferred_element_type=F32)
    mask = mask_ref[...].astype(F32).T
    lanes = lax.broadcasted_iota(I32, mask.shape, 1)
    parts = []
    for t in range(tiles):
        part = slice(t * TILE, (t + 1) * TILE)
        column = jnp.sum(jnp.where(lanes == step * tiles + t, mask, 0.0), axis=1, keepdims=True)
        trans = trans_ref[:, part].astype(F32)
        weights = trans * trans * ivar_ref[:, part].astype(F32) * column
        parts.append((weights * moved[:, part]).astype(BF16))
    weighted = jnp.concatenate(parts, axis=1)

    half, width = own_ref.shape
    core = lax.axis_index("c")
    own_ref[...] = jnp.dot(
        block_of(coef_t_ref, core, half), weighted, preferred_element_type=F32
    )
    other = jnp.dot(block_of(coef_t_ref, 1 - core, half), weighted, preferred_element_type=F32)
    for i in range(other_ref.shape[1] // width):

        @pl.when(step == i)
        def _():
            other_ref[:, i * width : (i + 1) * width] = other

    term = lax.dot_general(
        basis_ref[...], weighted, (((1,), (1,)), ((), ())), preferred_element_type=F32
    )

    @pl.when(step == 0)
    def _():
        term_ref[...] = term

    @pl.when(step > 0)
    def _():
        term_ref[...] += term

    @pl.when(step == pl.num_programs(0) - 1)
    def _():
        encode(other_ref[...], other_codes_ref)
        encode(term_ref[...], term_codes_ref)


def encode(total, out_ref):
    cols = total.shape[1]
    largest = jnp.max(jnp.abs(total), axis=1, keepdims=True) * 2.0**-BASE
    scale = jnp.full_like(largest, 2.0**-BASE)
    rung = jnp.zeros_like(largest)
    for bit in RUNG_BITS:
        fits = largest * 2.0**bit <= LARGEST
        largest = jnp.where(fits, largest * 2.0**bit, largest)
        scale = jnp.where(fits, scale * 2.0**bit, scale)
        rung = jnp.where(fits, rung + bit, rung)
    out_ref[:, :cols] = jnp.round(total * scale).astype(I32).astype(I16)
    rungs = jnp.broadcast_to(rung, (total.shape[0], TILE))
    out_ref[:, cols:] = rungs.astype(I32).astype(I16)


def decode(code_ref):
    cols = code_ref.shape[1] - TILE
    rung = code_ref[:, cols:].astype(I32)
    inverse = jnp.full(rung.shape, 2.0**BASE, F32)
    for bit in RUNG_BITS:
        inverse = inverse * jnp.where((rung & bit) != 0, F32(2.0**-bit), F32(1.0))
    return jnp.concatenate(
        [
            code_ref[:, t * TILE : (t + 1) * TILE].astype(I32).astype(F32) * inverse
            for t in range(cols // TILE)
        ],
        axis=1,
    )


def spread_kernel(in_ref, out_ref):
    for i in range(out_ref.shape[0]):
        out_ref[i] = in_ref[...]


def spread_pair_kernel(mine_ref, other_ref, out_ref):
    mine, other = mine_ref[...].astype(F32), other_ref[...].astype(F32)
    first = lax.axis_index("yh") == 0
    pair = [jnp.where(first, mine, other), jnp.where(first, other, mine)]
    pair = jnp.concatenate(pair, axis=0).astype(BF16)
    for i in range(out_ref.shape[0]):
        out_ref[i] = pair


def add_kernel(own_ref, both_ref, out_ref):
    n = own_ref.shape[0]
    came = pl.ds(pl.multiple_of((1 - lax.axis_index("c")) * n, n), n)
    encode(own_ref[...] + decode(both_ref.at[came]), out_ref)


def part_of(ref, i, count):
    return ref.at[i * count : (i + 1) * count]


def halve_kernel(in_ref, keep_ref, give_ref):
    n = keep_ref.shape[0]
    total = sum(decode(part_of(in_ref, i, 2 * n)) for i in range(in_ref.shape[0] // (2 * n)))
    first = lax.axis_index("yh") == 0
    low, high = total[:n], total[n:]
    keep_ref[...] = jnp.where(first, low, high)
    encode(jnp.where(first, high, low), give_ref)


def last_kernel(divisor, mine_ref, came_ref, out_ref):
    out_ref[...] = (mine_ref[...] + decode(came_ref)) * (1.0 / divisor)


def coef_kernel(divisor, in_ref, out_ref):
    n = out_ref.shape[0]
    total = sum(decode(part_of(in_ref, i, n)) for i in range(in_ref.shape[0] // n))
    out_ref[...] = total * (1.0 / divisor)


def body(transmission, inverse_var, pixel_mask, coef, basis, coef_tangent, basis_tangent):
    rows, cols = transmission.shape
    rank = basis.shape[0]
    half, mine, ours = rank // 2, rank // 32, rank // 16
    exposures, pixels = rows * 32, cols * 16

    small = lambda kernel, *shapes: pl.pallas_call(
        kernel,
        out_shape=[jax.ShapeDtypeStruct(*shape) for shape in shapes],
        compiler_params=pltpu.CompilerParams(vmem_limit_bytes=8 << 20),
    )
    exchange = lambda value, axis: lax.all_to_all(value, axis, 0, 0, tiled=True)

    across = partner(basis_tangent, "yh", 1)
    [pair] = small(spread_pair_kernel, ((8, 2 * mine, cols), BF16))(in_hbm(basis_tangent), across)
    [tangent] = small(spread_kernel, ((16, ours, rows), BF16))(in_hbm(coef_tangent.T))
    pair, tangent = lax.optimization_barrier((pair, tangent))
    arrived = exchange(pair, "z").reshape(half, cols)

    arrived, tangent = lax.optimization_barrier((arrived, tangent))
    tangent = exchange(tangent, ("x", "yl")).reshape(rank, rows)
    full = lax.all_gather(arrived, "c", axis=0, tiled=True)

    width = cols // 2
    whole = lambda *shape: pl.BlockSpec(shape, lambda i: (0,) * len(shape))
    tall = lambda n: pl.BlockSpec((n, width), lambda i: (0, i))
    own, codes, terms = pl.pallas_call(
        fused_kernel,
        grid=(cols // width,),
        in_specs=[
            tall(rows), tall(rows), whole(cols // TILE, rows), whole(rank, rows),
            whole(rows, rank), tall(rank), tall(rank),
        ],
        out_specs=[tall(half), whole(half, cols + TILE), whole(rank, rows + TILE)],
        out_shape=[
            jax.ShapeDtypeStruct((half, cols), F32),
            jax.ShapeDtypeStruct((half, cols + TILE), I16),
            jax.ShapeDtypeStruct((rank, rows + TILE), I16),
        ],
        scratch_shapes=[
            pltpu.VMEM((rows, rank), BF16), pltpu.VMEM((rank, rows), BF16),
            pltpu.VMEM((half, cols), F32), pltpu.VMEM((rank, rows), F32),
        ],
        compiler_params=pltpu.CompilerParams(vmem_limit_bytes=32 << 20),
        cost_estimate=pl.CostEstimate(
            flops=8 * rows * cols * rank, bytes_accessed=6 * rows * cols, transcendentals=0
        ),
    )(
        in_hbm(transmission), in_hbm(inverse_var), in_hbm(pixel_mask.T), tangent,
        in_hbm(coef), full, in_hbm(basis),
    )

    terms = exchange(terms.reshape(16, ours, rows + TILE), ("x", "yl")).reshape(rank, rows + TILE)
    codes = lax.all_gather(codes, "c", axis=0, tiled=True)
    [codes] = small(add_kernel, ((half, cols + TILE), I16))(own, codes)
    codes, terms = lax.optimization_barrier((codes, terms))

    codes = exchange(codes.reshape(8, 2 * mine, cols + TILE), "z").reshape(half, cols + TILE)
    codes, terms = lax.optimization_barrier((codes, terms))
    keep, give = small(halve_kernel, ((mine, cols), F32), ((mine, cols + TILE), I16))(codes)
    [basis_grad] = small(
        functools.partial(last_kernel, math.sqrt(exposures)), ((mine, cols), F32)
    )(keep, partner(give, "yh", 1))
    [coef_grad] = small(
        functools.partial(coef_kernel, math.sqrt(pixels)), ((ours, rows), F32)
    )(terms)
    return (coef_grad.T, basis_grad)


def solution(mesh):
    fine = Mesh(mesh.devices.reshape(2, 8, 2, 4, 4), ("yh", "z", "c", "x", "yl"))
    exp, pix = ("yh", "z", "c"), ("x", "yl")
    placed = (
        P(exp, pix),
        P(exp, pix),
        P(exp, pix),
        P(exp, None),
        P(None, pix),
        P(exp, pix),
        P(exp, pix),
    )
    return jax.shard_map(
        body,
        mesh=fine,
        in_specs=placed,
        out_specs=(P(exp, pix), P(exp, pix)),
        check_vma=False,
    )
```

```python
import functools
import math

import jax
import jax.numpy as jnp
from jax import lax
from jax.experimental import pallas as pl
from jax.experimental.pallas import tpu as pltpu
from jax.sharding import Mesh
from jax.sharding import PartitionSpec as P

TILE = 128
BF16, F32, I16, I32 = jnp.bfloat16, jnp.float32, jnp.int16, jnp.int32
HALVINGS = (("yl", 1), ("x", 1), ("yl", 2), ("x", 2))
BASE, RUNG_BITS, LARGEST = 14, (64, 32, 16, 8, 4, 2, 1), 32767.0


def partner(value, axis, flip):
    return lax.ppermute(value, axis, [(i, i ^ flip) for i in range(lax.axis_size(axis))])


def in_hbm(value):
    return pltpu.with_memory_space_constraint(value, pltpu.HBM)


def block_of(ref, which, count):
    return ref[pl.ds(pl.multiple_of(which * count, count), count), :]


def fused_kernel(
    trans_ref, ivar_ref, mask_ref, tangent_ref, coef_ref, full_ref, basis_ref,
    own_ref, other_ref, kept_ref, given_ref, coef_p_ref, coef_t_ref,
):
    step = pl.program_id(0)

    @pl.when(step == 0)
    def _():
        rank = coef_ref.shape[1]
        take = lax.broadcasted_iota(I32, (rank, rank), 0)
        place = lax.broadcasted_iota(I32, (rank, rank), 1)
        low, mid, high = place & 7, place & 112, ((place >> 3) & 1) * 128 + ((place >> 7) & 1) * 8
        chosen = (take == low + mid + high).astype(BF16)
        coef = coef_ref[...]
        coef_p_ref[...] = jnp.dot(coef, chosen, preferred_element_type=F32).astype(BF16)
        coef_t_ref[...] = lax.dot_general(
            chosen, coef, (((0,), (1,)), ((), ())), preferred_element_type=F32
        ).astype(BF16)

    tiles = trans_ref.shape[1] // TILE
    x, y = lax.axis_index("x"), lax.axis_index("yl")
    count = basis_ref.shape[0] // 16
    basis = jnp.concatenate(
        [
            block_of(basis_ref, (x ^ (b + 2 * d)) * 4 + (y ^ (a + 2 * c)), count)
            for a in (0, 1)
            for b in (0, 1)
            for c in (0, 1)
            for d in (0, 1)
        ],
        axis=0,
    )
    moved = lax.dot_general(
        tangent_ref[...], basis, (((0,), (0,)), ((), ())), preferred_element_type=F32
    ) + jnp.dot(coef_p_ref[...], full_ref[...], preferred_element_type=F32)
    mask = mask_ref[...].astype(F32).T
    lanes = lax.broadcasted_iota(I32, mask.shape, 1)
    parts = []
    for t in range(tiles):
        part = slice(t * TILE, (t + 1) * TILE)
        column = jnp.sum(jnp.where(lanes == step * tiles + t, mask, 0.0), axis=1, keepdims=True)
        trans = trans_ref[:, part].astype(F32)
        weights = trans * trans * ivar_ref[:, part].astype(F32) * column
        parts.append((weights * moved[:, part]).astype(BF16))
    weighted = jnp.concatenate(parts, axis=1)

    half = own_ref.shape[0]
    core = lax.axis_index("c")
    for out, which in ((own_ref, core), (other_ref, 1 - core)):
        rows = block_of(coef_t_ref, which, half)
        out[...] = jnp.dot(rows, weighted, preferred_element_type=F32)
    term = lax.dot_general(
        basis, weighted, (((1,), (1,)), ((), ())), preferred_element_type=F32
    )
    n = kept_ref.shape[0]

    @pl.when(step == 0)
    def _():
        kept_ref[...] = term[:n]
        given_ref[...] = term[n:]

    @pl.when(step > 0)
    def _():
        kept_ref[...] += term[:n]
        given_ref[...] += term[n:]


def encode(total, out_ref):
    cols = total.shape[1]
    largest = jnp.max(jnp.abs(total), axis=1, keepdims=True) * 2.0**-BASE
    scale = jnp.full_like(largest, 2.0**-BASE)
    rung = jnp.zeros_like(largest)
    for bit in RUNG_BITS:
        fits = largest * 2.0**bit <= LARGEST
        largest = jnp.where(fits, largest * 2.0**bit, largest)
        scale = jnp.where(fits, scale * 2.0**bit, scale)
        rung = jnp.where(fits, rung + bit, rung)
    out_ref[:, :cols] = jnp.round(total * scale).astype(I32).astype(I16)
    rungs = jnp.broadcast_to(rung, (total.shape[0], TILE))
    out_ref[:, cols:] = rungs.astype(I32).astype(I16)


def decode(code_ref):
    cols = code_ref.shape[1] - TILE
    rung = code_ref[:, cols:].astype(I32)
    inverse = jnp.full(rung.shape, 2.0**BASE, F32)
    for bit in RUNG_BITS:
        inverse = inverse * jnp.where((rung & bit) != 0, F32(2.0**-bit), F32(1.0))
    return jnp.concatenate(
        [
            code_ref[:, t * TILE : (t + 1) * TILE].astype(I32).astype(F32) * inverse
            for t in range(cols // TILE)
        ],
        axis=1,
    )


def join_kernel(mine_ref, came_ref, out_ref):
    n = mine_ref.shape[0]
    out_ref[:n] = mine_ref[...]
    out_ref[n:] = came_ref[...]


def spread_pair_kernel(mine_ref, other_ref, out_ref):
    mine, other = mine_ref[...].astype(F32), other_ref[...].astype(F32)
    first = lax.axis_index("yh") == 0
    pair = [jnp.where(first, mine, other), jnp.where(first, other, mine)]
    pair = jnp.concatenate(pair, axis=0).astype(BF16)
    for i in range(out_ref.shape[0]):
        out_ref[i] = pair


def pack_kernel(term_ref, out_ref):
    encode(term_ref[...], out_ref)


def add_kernel(own_ref, both_ref, out_ref):
    n = own_ref.shape[0]
    came = pl.ds(pl.multiple_of((1 - lax.axis_index("c")) * n, n), n)
    encode(own_ref[...] + decode(both_ref.at[came]), out_ref)


def part_of(ref, i, count):
    return ref.at[i * count : (i + 1) * count]


def halve_kernel(in_ref, keep_ref, give_ref):
    n = keep_ref.shape[0]
    total = sum(decode(part_of(in_ref, i, 2 * n)) for i in range(in_ref.shape[0] // (2 * n)))
    first = lax.axis_index("yh") == 0
    low, high = total[:n], total[n:]
    keep_ref[...] = jnp.where(first, low, high)
    encode(jnp.where(first, high, low), give_ref)


def last_kernel(divisor, mine_ref, came_ref, out_ref):
    out_ref[...] = (mine_ref[...] + decode(came_ref)) * (1.0 / divisor)


def body(transmission, inverse_var, pixel_mask, coef, basis, coef_tangent, basis_tangent):
    rows, cols = transmission.shape
    rank = basis.shape[0]
    half, mine, ours = rank // 2, rank // 32, rank // 16
    exposures, pixels = rows * 32, cols * 16

    small = lambda kernel, *shapes: pl.pallas_call(
        kernel,
        out_shape=[jax.ShapeDtypeStruct(*shape) for shape in shapes],
        compiler_params=pltpu.CompilerParams(vmem_limit_bytes=8 << 20),
    )
    exchange = lambda value, axis: lax.all_to_all(value, axis, 0, 0, tiled=True)

    def joined(tangent, stage):
        came = partner(tangent, *stage)
        [tangent] = small(join_kernel, ((2 * tangent.shape[0], rows), BF16))(tangent, came)
        return tangent

    across = partner(basis_tangent, "yh", 1)
    *doublings, first = HALVINGS
    tangent = joined(coef_tangent.T, first)
    [pair] = small(spread_pair_kernel, ((8, 2 * mine, cols), BF16))(in_hbm(basis_tangent), across)
    pair, tangent = lax.optimization_barrier((pair, tangent))

    arrived = exchange(pair, "z").reshape(half, cols)
    full = lax.all_gather(arrived, "c", axis=0, tiled=True)
    for stage in reversed(doublings):
        tangent = joined(tangent, stage)

    width = cols // 2
    whole = lambda *shape: pl.BlockSpec(shape, lambda i: (0,) * len(shape))
    tall = lambda n: pl.BlockSpec((n, width), lambda i: (0, i))
    own, other, kept, given = pl.pallas_call(
        fused_kernel,
        grid=(cols // width,),
        in_specs=[
            tall(rows), tall(rows), whole(cols // TILE, rows), whole(rank, rows),
            whole(rows, rank), tall(rank), tall(rank),
        ],
        out_specs=[tall(half), tall(half), whole(half, rows), whole(half, rows)],
        out_shape=[
            jax.ShapeDtypeStruct((half, cols), F32),
            jax.ShapeDtypeStruct((half, cols), F32),
            jax.ShapeDtypeStruct((half, rows), F32),
            jax.ShapeDtypeStruct((half, rows), F32),
        ],
        scratch_shapes=[pltpu.VMEM((rows, rank), BF16), pltpu.VMEM((rank, rows), BF16)],
        compiler_params=pltpu.CompilerParams(vmem_limit_bytes=32 << 20),
        cost_estimate=pl.CostEstimate(
            flops=8 * rows * cols * rank, bytes_accessed=6 * rows * cols, transcendentals=0
        ),
    )(*map(in_hbm, (transmission, inverse_var)), pixel_mask.T, tangent, coef, full, basis)

    [codes] = small(pack_kernel, ((half, cols + TILE), I16))(other)
    codes = lax.all_gather(codes, "c", axis=0, tiled=True)
    [codes] = small(add_kernel, ((half, cols + TILE), I16))(own, codes)
    codes = exchange(codes.reshape(8, 2 * mine, cols + TILE), "z").reshape(half, cols + TILE)
    keep, give = small(halve_kernel, ((mine, cols), F32), ((mine, cols + TILE), I16))(codes)

    for axis, flip in HALVINGS:
        if (axis, flip) == HALVINGS[-1]:
            given, give = lax.optimization_barrier((given, give))
        total = kept + partner(given, axis, flip)
        n = total.shape[0] // 2
        kept, given = total[:n], total[n:]
    coef_grad = total * (1.0 / math.sqrt(pixels))
    [basis_grad] = small(
        functools.partial(last_kernel, math.sqrt(exposures)), ((mine, cols), F32)
    )(keep, partner(give, "yh", 1))
    return (coef_grad.T, basis_grad)


def solution(mesh):
    fine = Mesh(mesh.devices.reshape(2, 8, 2, 4, 4), ("yh", "z", "c", "x", "yl"))
    exp, pix = ("yh", "z", "c"), ("x", "yl")
    placed = (
        P(exp, pix),
        P(exp, pix),
        P(exp, pix),
        P(exp, None),
        P(None, pix),
        P(exp, pix),
        P(exp, pix),
    )
    return jax.shard_map(
        body,
        mesh=fine,
        in_specs=placed,
        out_specs=(P(exp, pix), P(exp, pix)),
        check_vma=False,
    )
```

```python
import functools
import math

import jax
import jax.numpy as jnp
from jax import lax
from jax.experimental import pallas as pl
from jax.experimental.pallas import tpu as pltpu
from jax.sharding import Mesh
from jax.sharding import PartitionSpec as P

TILE = 128
BF16, F32, I16, I32 = jnp.bfloat16, jnp.float32, jnp.int16, jnp.int32
BASE, RUNG_BITS, LARGEST = 14, (64, 32, 16, 8, 4, 2, 1), 32767.0


def partner(value, axis, flip):
    return lax.ppermute(value, axis, [(i, i ^ flip) for i in range(lax.axis_size(axis))])


def in_hbm(value):
    return pltpu.with_memory_space_constraint(value, pltpu.HBM)


def block_of(ref, which, count):
    return ref[pl.ds(pl.multiple_of(which * count, count), count), :]


def fused_kernel(
    trans_ref, ivar_ref, mask_ref, tangent_ref, coef_ref, full_ref, basis_ref,
    own_ref, other_ref, term_ref, coef_p_ref, coef_t_ref, trans_here, ivar_here, arrivals,
):
    step = pl.program_id(0)
    steps, _, width = trans_here.shape

    def arrival(k, i):
        source, here = ((trans_ref, trans_here), (ivar_ref, ivar_here))[k]
        return pltpu.make_async_copy(
            source.at[:, i * width : (i + 1) * width], here.at[i], arrivals.at[k, i]
        )

    @pl.when(step == 0)
    def _():
        for i in range(steps):
            arrival(0, i).start()
            arrival(1, i).start()
        rank = coef_ref.shape[1]
        take = lax.broadcasted_iota(I32, (rank, rank), 0)
        place = lax.broadcasted_iota(I32, (rank, rank), 1)
        low, mid, high = place & 7, place & 112, ((place >> 3) & 1) * 128 + ((place >> 7) & 1) * 8
        chosen = (take == low + mid + high).astype(BF16)
        coef = coef_ref[...]
        coef_p_ref[...] = jnp.dot(coef, chosen, preferred_element_type=F32).astype(BF16)
        coef_t_ref[...] = lax.dot_general(
            chosen, coef, (((0,), (1,)), ((), ())), preferred_element_type=F32
        ).astype(BF16)

    tiles = width // TILE
    moved = lax.dot_general(
        tangent_ref[...], basis_ref[...], (((0,), (0,)), ((), ())), preferred_element_type=F32
    ) + jnp.dot(coef_p_ref[...], full_ref[...], preferred_element_type=F32)
    mask = mask_ref[...].astype(F32).T
    lanes = lax.broadcasted_iota(I32, mask.shape, 1)
    for i in range(steps):

        @pl.when(step == i)
        def _():
            arrival(0, i).wait()
            arrival(1, i).wait()

    parts = []
    for t in range(tiles):
        part = slice(t * TILE, (t + 1) * TILE)
        column = jnp.sum(jnp.where(lanes == step * tiles + t, mask, 0.0), axis=1, keepdims=True)
        trans = trans_here[step, :, part].astype(F32)
        weights = trans * trans * ivar_here[step, :, part].astype(F32) * column
        parts.append((weights * moved[:, part]).astype(BF16))
    weighted = jnp.concatenate(parts, axis=1)

    half = own_ref.shape[0]
    core = lax.axis_index("c")
    for out, which in ((own_ref, core), (other_ref, 1 - core)):
        rows = block_of(coef_t_ref, which, half)
        out[...] = jnp.dot(rows, weighted, preferred_element_type=F32)
    term = lax.dot_general(
        basis_ref[...], weighted, (((1,), (1,)), ((), ())), preferred_element_type=F32
    )

    @pl.when(step == 0)
    def _():
        term_ref[...] = term

    @pl.when(step > 0)
    def _():
        term_ref[...] += term


def encode(total, out_ref):
    cols = total.shape[1]
    largest = jnp.max(jnp.abs(total), axis=1, keepdims=True) * 2.0**-BASE
    scale = jnp.full_like(largest, 2.0**-BASE)
    rung = jnp.zeros_like(largest)
    for bit in RUNG_BITS:
        fits = largest * 2.0**bit <= LARGEST
        largest = jnp.where(fits, largest * 2.0**bit, largest)
        scale = jnp.where(fits, scale * 2.0**bit, scale)
        rung = jnp.where(fits, rung + bit, rung)
    out_ref[:, :cols] = jnp.round(total * scale).astype(I32).astype(I16)
    rungs = jnp.broadcast_to(rung, (total.shape[0], TILE))
    out_ref[:, cols:] = rungs.astype(I32).astype(I16)


def decode(code_ref):
    cols = code_ref.shape[1] - TILE
    rung = code_ref[:, cols:].astype(I32)
    inverse = jnp.full(rung.shape, 2.0**BASE, F32)
    for bit in RUNG_BITS:
        inverse = inverse * jnp.where((rung & bit) != 0, F32(2.0**-bit), F32(1.0))
    return jnp.concatenate(
        [
            code_ref[:, t * TILE : (t + 1) * TILE].astype(I32).astype(F32) * inverse
            for t in range(cols // TILE)
        ],
        axis=1,
    )


def spread_kernel(in_ref, out_ref, sent):
    copies = [
        pltpu.make_async_copy(in_ref, out_ref.at[i], sent.at[i]) for i in range(out_ref.shape[0])
    ]
    for copy in copies:
        copy.start()
    for copy in copies:
        copy.wait()


def spread_pair_kernel(mine_ref, other_ref, out_ref):
    mine, other = mine_ref[...].astype(F32), other_ref[...].astype(F32)
    first = lax.axis_index("yh") == 0
    pair = [jnp.where(first, mine, other), jnp.where(first, other, mine)]
    pair = jnp.concatenate(pair, axis=0).astype(BF16)
    for i in range(out_ref.shape[0]):
        out_ref[i] = pair


def pack_kernel(term_ref, out_ref):
    encode(term_ref[...], out_ref)


def add_kernel(own_ref, both_ref, out_ref):
    n = own_ref.shape[0]
    came = pl.ds(pl.multiple_of((1 - lax.axis_index("c")) * n, n), n)
    encode(own_ref[...] + decode(both_ref.at[came]), out_ref)


def part_of(ref, i, count):
    return ref.at[i * count : (i + 1) * count]


def halve_kernel(in_ref, keep_ref, give_ref):
    n = keep_ref.shape[0]
    total = sum(decode(part_of(in_ref, i, 2 * n)) for i in range(in_ref.shape[0] // (2 * n)))
    first = lax.axis_index("yh") == 0
    low, high = total[:n], total[n:]
    keep_ref[...] = jnp.where(first, low, high)
    encode(jnp.where(first, high, low), give_ref)


def last_kernel(divisor, mine_ref, came_ref, out_ref):
    out_ref[...] = (mine_ref[...] + decode(came_ref)) * (1.0 / divisor)


def coef_kernel(divisor, in_ref, out_ref):
    n = out_ref.shape[0]
    total = sum(decode(part_of(in_ref, i, n)) for i in range(in_ref.shape[0] // n))
    out_ref[...] = total * (1.0 / divisor)


def body(transmission, inverse_var, pixel_mask, coef, basis, coef_tangent, basis_tangent):
    rows, cols = transmission.shape
    rank = basis.shape[0]
    half, mine, ours = rank // 2, rank // 32, rank // 16
    exposures, pixels = rows * 32, cols * 16

    small = lambda kernel, *shapes: pl.pallas_call(
        kernel,
        out_shape=[jax.ShapeDtypeStruct(*shape) for shape in shapes],
        compiler_params=pltpu.CompilerParams(vmem_limit_bytes=8 << 20),
    )
    exchange = lambda value, axis: lax.all_to_all(value, axis, 0, 0, tiled=True)

    across = partner(basis_tangent, "yh", 1)
    tangent = pl.pallas_call(
        spread_kernel,
        out_shape=jax.ShapeDtypeStruct((16, ours, rows), BF16),
        out_specs=pl.BlockSpec(memory_space=pl.ANY),
        scratch_shapes=[pltpu.SemaphoreType.DMA((16,))],
        compiler_params=pltpu.CompilerParams(vmem_limit_bytes=8 << 20),
    )(in_hbm(coef_tangent.T))
    tangent = exchange(tangent, ("x", "yl")).reshape(rank, rows)
    across, tangent = lax.optimization_barrier((across, tangent))

    [pair] = small(spread_pair_kernel, ((8, 2 * mine, cols), BF16))(in_hbm(basis_tangent), across)
    arrived = exchange(pair, "z").reshape(half, cols)
    full = lax.all_gather(arrived, "c", axis=0, tiled=True)

    width = cols // 2
    anywhere = pl.BlockSpec(memory_space=pl.ANY)
    whole = lambda *shape: pl.BlockSpec(shape, lambda i: (0,) * len(shape))
    tall = lambda n: pl.BlockSpec((n, width), lambda i: (0, i))
    own, other, term = pl.pallas_call(
        fused_kernel,
        grid=(cols // width,),
        in_specs=[
            anywhere, anywhere, whole(cols // TILE, rows), whole(rank, rows),
            whole(rows, rank), tall(rank), tall(rank),
        ],
        out_specs=[tall(half), tall(half), whole(rank, rows)],
        out_shape=[
            jax.ShapeDtypeStruct((half, cols), F32),
            jax.ShapeDtypeStruct((half, cols), F32),
            jax.ShapeDtypeStruct((rank, rows), F32),
        ],
        scratch_shapes=[
            pltpu.VMEM((rows, rank), BF16),
            pltpu.VMEM((rank, rows), BF16),
            pltpu.VMEM((cols // width, rows, width), BF16),
            pltpu.VMEM((cols // width, rows, width), BF16),
            pltpu.SemaphoreType.DMA((2, cols // width)),
        ],
        compiler_params=pltpu.CompilerParams(vmem_limit_bytes=32 << 20),
        cost_estimate=pl.CostEstimate(
            flops=8 * rows * cols * rank, bytes_accessed=6 * rows * cols, transcendentals=0
        ),
    )(*map(in_hbm, (transmission, inverse_var)), pixel_mask.T, tangent, coef, full, basis)

    [codes] = small(pack_kernel, ((half, cols + TILE), I16))(other)
    codes = lax.all_gather(codes, "c", axis=0, tiled=True)
    [codes] = small(add_kernel, ((half, cols + TILE), I16))(own, codes)
    terms = pl.pallas_call(
        pack_kernel,
        grid=(4,),
        in_specs=[pl.BlockSpec((rank // 4, rows), lambda i: (i, 0))],
        out_specs=pl.BlockSpec((rank // 4, rows + TILE), lambda i: (i, 0)),
        out_shape=jax.ShapeDtypeStruct((rank, rows + TILE), I16),
        compiler_params=pltpu.CompilerParams(vmem_limit_bytes=8 << 20),
    )(term)
    codes, terms = lax.optimization_barrier((codes, terms))
    codes = exchange(codes.reshape(8, 2 * mine, cols + TILE), "z").reshape(half, cols + TILE)

    keep, give = small(halve_kernel, ((mine, cols), F32), ((mine, cols + TILE), I16))(codes)
    [basis_grad] = small(
        functools.partial(last_kernel, math.sqrt(exposures)), ((mine, cols), F32)
    )(keep, partner(give, "yh", 1))
    terms = exchange(terms.reshape(16, ours, rows + TILE), ("x", "yl")).reshape(rank, rows + TILE)
    [coef_grad] = small(
        functools.partial(coef_kernel, math.sqrt(pixels)), ((ours, rows), F32)
    )(terms)
    return (coef_grad.T, basis_grad)


def solution(mesh):
    fine = Mesh(mesh.devices.reshape(2, 8, 2, 4, 4), ("yh", "z", "c", "x", "yl"))
    exp, pix = ("yh", "z", "c"), ("x", "yl")
    placed = (
        P(exp, pix),
        P(exp, pix),
        P(exp, pix),
        P(exp, None),
        P(None, pix),
        P(exp, pix),
        P(exp, pix),
    )
    return jax.shard_map(
        body,
        mesh=fine,
        in_specs=placed,
        out_specs=(P(exp, pix), P(exp, pix)),
        check_vma=False,
    )
```

```python
import functools
import math

import jax
import jax.numpy as jnp
from jax import lax
from jax.experimental import pallas as pl
from jax.experimental.pallas import tpu as pltpu
from jax.sharding import Mesh
from jax.sharding import PartitionSpec as P

TILE = 128
BF16, F32, I16, I32 = jnp.bfloat16, jnp.float32, jnp.int16, jnp.int32
BASE, RUNG_BITS, LARGEST = 14, (64, 32, 16, 8, 4, 2, 1), 32767.0


def partner(value, axis, flip):
    return lax.ppermute(value, axis, [(i, i ^ flip) for i in range(lax.axis_size(axis))])


def in_hbm(value):
    return pltpu.with_memory_space_constraint(value, pltpu.HBM)


def block_of(ref, which, count):
    return ref[pl.ds(pl.multiple_of(which * count, count), count), :]


def fused_kernel(
    trans_ref, ivar_ref, mask_ref, tangent_ref, coef_ref, full_ref, basis_ref,
    own_ref, other_ref, term_ref, coef_p_ref, coef_t_ref,
):
    step = pl.program_id(0)

    @pl.when(step == 0)
    def _():
        rank = coef_ref.shape[1]
        take = lax.broadcasted_iota(I32, (rank, rank), 0)
        place = lax.broadcasted_iota(I32, (rank, rank), 1)
        core, row = (place >> 7) * 8, place & 7
        by_column = (take == ((place >> 3) & 15) * 16 + core + row).astype(BF16)
        by_row = (take == ((place >> 3) & 1) * 128 + (place & 112) + core + row).astype(BF16)
        coef = coef_ref[...]
        coef_p_ref[...] = jnp.dot(coef, by_column, preferred_element_type=F32).astype(BF16)
        coef_t_ref[...] = lax.dot_general(
            by_row, coef, (((0,), (1,)), ((), ())), preferred_element_type=F32
        ).astype(BF16)

    tiles = trans_ref.shape[1] // TILE
    moved = lax.dot_general(
        tangent_ref[...], basis_ref[...], (((0,), (0,)), ((), ())), preferred_element_type=F32
    ) + jnp.dot(coef_p_ref[...], full_ref[...], preferred_element_type=F32)
    mask = mask_ref[...].astype(F32).T
    lanes = lax.broadcasted_iota(I32, mask.shape, 1)
    parts = []
    for t in range(tiles):
        part = slice(t * TILE, (t + 1) * TILE)
        column = jnp.sum(jnp.where(lanes == step * tiles + t, mask, 0.0), axis=1, keepdims=True)
        trans = trans_ref[:, part].astype(F32)
        weights = trans * trans * ivar_ref[:, part].astype(F32) * column
        parts.append((weights * moved[:, part]).astype(BF16))
    weighted = jnp.concatenate(parts, axis=1)

    half = own_ref.shape[0]
    core = lax.axis_index("c")
    for out, which in ((own_ref, core), (other_ref, 1 - core)):
        rows = block_of(coef_t_ref, which, half)
        out[...] = jnp.dot(rows, weighted, preferred_element_type=F32)
    term = lax.dot_general(
        basis_ref[...], weighted, (((1,), (1,)), ((), ())), preferred_element_type=F32
    )

    @pl.when(step == 0)
    def _():
        term_ref[...] = term

    @pl.when(step > 0)
    def _():
        term_ref[...] += term


def encode(total, out_ref):
    cols = total.shape[1]
    largest = jnp.max(jnp.abs(total), axis=1, keepdims=True) * 2.0**-BASE
    scale = jnp.full_like(largest, 2.0**-BASE)
    rung = jnp.zeros_like(largest)
    for bit in RUNG_BITS:
        fits = largest * 2.0**bit <= LARGEST
        largest = jnp.where(fits, largest * 2.0**bit, largest)
        scale = jnp.where(fits, scale * 2.0**bit, scale)
        rung = jnp.where(fits, rung + bit, rung)
    out_ref[:, :cols] = jnp.round(total * scale).astype(I32).astype(I16)
    rungs = jnp.broadcast_to(rung, (total.shape[0], TILE))
    out_ref[:, cols:] = rungs.astype(I32).astype(I16)


def decode(code_ref):
    cols = code_ref.shape[1] - TILE
    rung = code_ref[:, cols:].astype(I32)
    inverse = jnp.full(rung.shape, 2.0**BASE, F32)
    for bit in RUNG_BITS:
        inverse = inverse * jnp.where((rung & bit) != 0, F32(2.0**-bit), F32(1.0))
    return jnp.concatenate(
        [
            code_ref[:, t * TILE : (t + 1) * TILE].astype(I32).astype(F32) * inverse
            for t in range(cols // TILE)
        ],
        axis=1,
    )


def spread_kernel(in_ref, out_ref):
    for i in range(out_ref.shape[0]):
        out_ref[i] = in_ref[...]


def pack_kernel(term_ref, out_ref):
    encode(term_ref[...], out_ref)


def add_kernel(own_ref, both_ref, out_ref):
    n = own_ref.shape[0]
    came = pl.ds(pl.multiple_of((1 - lax.axis_index("c")) * n, n), n)
    encode(own_ref[...] + decode(both_ref.at[came]), out_ref)


def part_of(ref, i, count):
    return ref.at[i * count : (i + 1) * count]


def halve_kernel(in_ref, keep_ref, give_ref):
    n = keep_ref.shape[0]
    total = sum(decode(part_of(in_ref, i, 2 * n)) for i in range(in_ref.shape[0] // (2 * n)))
    first = lax.axis_index("yh") == 0
    low, high = total[:n], total[n:]
    keep_ref[...] = jnp.where(first, low, high)
    encode(jnp.where(first, high, low), give_ref)


def last_kernel(divisor, mine_ref, came_ref, out_ref):
    out_ref[...] = (mine_ref[...] + decode(came_ref)) * (1.0 / divisor)


def coef_kernel(divisor, in_ref, out_ref):
    n = out_ref.shape[0]
    total = sum(decode(part_of(in_ref, i, n)) for i in range(in_ref.shape[0] // n))
    out_ref[...] = total * (1.0 / divisor)


def body(transmission, inverse_var, pixel_mask, coef, basis, coef_tangent, basis_tangent):
    rows, cols = transmission.shape
    rank = basis.shape[0]
    half, mine, ours = rank // 2, rank // 32, rank // 16
    exposures, pixels = rows * 32, cols * 16

    small = lambda kernel, *shapes: pl.pallas_call(
        kernel,
        out_shape=[jax.ShapeDtypeStruct(*shape) for shape in shapes],
        compiler_params=pltpu.CompilerParams(vmem_limit_bytes=8 << 20),
    )
    exchange = lambda value, axis: lax.all_to_all(value, axis, 0, 0, tiled=True)

    [tangent] = small(spread_kernel, ((16, ours, rows), BF16))(coef_tangent.T)
    [spread] = small(spread_kernel, ((16, mine, cols), BF16))(in_hbm(basis_tangent))
    tangent, spread = lax.optimization_barrier((tangent, spread))
    tangent = exchange(tangent, ("x", "yl")).reshape(rank, rows)
    spread, tangent = lax.optimization_barrier((spread, tangent))
    arrived = exchange(spread, ("yh", "z")).reshape(half, cols)
    full = lax.all_gather(arrived, "c", axis=0, tiled=True)

    width = cols // 2
    whole = lambda *shape: pl.BlockSpec(shape, lambda i: (0,) * len(shape))
    tall = lambda n: pl.BlockSpec((n, width), lambda i: (0, i))
    own, other, term = pl.pallas_call(
        fused_kernel,
        grid=(cols // width,),
        in_specs=[
            tall(rows), tall(rows), whole(cols // TILE, rows), whole(rank, rows),
            whole(rows, rank), tall(rank), tall(rank),
        ],
        out_specs=[tall(half), tall(half), whole(rank, rows)],
        out_shape=[
            jax.ShapeDtypeStruct((half, cols), F32),
            jax.ShapeDtypeStruct((half, cols), F32),
            jax.ShapeDtypeStruct((rank, rows), F32),
        ],
        scratch_shapes=[pltpu.VMEM((rows, rank), BF16), pltpu.VMEM((rank, rows), BF16)],
        compiler_params=pltpu.CompilerParams(vmem_limit_bytes=32 << 20),
        cost_estimate=pl.CostEstimate(
            flops=8 * rows * cols * rank, bytes_accessed=6 * rows * cols, transcendentals=0
        ),
    )(transmission, in_hbm(inverse_var), pixel_mask.T, tangent, coef, full, basis)

    [codes] = small(pack_kernel, ((half, cols + TILE), I16))(other)
    codes = lax.all_gather(codes, "c", axis=0, tiled=True)
    [codes] = small(add_kernel, ((half, cols + TILE), I16))(own, codes)
    [terms] = small(pack_kernel, ((rank, rows + TILE), I16))(term)
    codes, terms = lax.optimization_barrier((codes, terms))
    codes = exchange(codes.reshape(8, 2 * mine, cols + TILE), "z").reshape(half, cols + TILE)

    keep, give = small(halve_kernel, ((mine, cols), F32), ((mine, cols + TILE), I16))(codes)
    [basis_grad] = small(
        functools.partial(last_kernel, math.sqrt(exposures)), ((mine, cols), F32)
    )(keep, partner(give, "yh", 1))
    terms = exchange(terms.reshape(16, ours, rows + TILE), ("x", "yl")).reshape(rank, rows + TILE)
    [coef_grad] = small(
        functools.partial(coef_kernel, math.sqrt(pixels)), ((ours, rows), F32)
    )(terms)
    return (coef_grad.T, basis_grad)


def solution(mesh):
    fine = Mesh(mesh.devices.reshape(2, 8, 2, 4, 4), ("yh", "z", "c", "x", "yl"))
    exp, pix = ("yh", "z", "c"), ("x", "yl")
    placed = (
        P(exp, pix),
        P(exp, pix),
        P(exp, pix),
        P(exp, None),
        P(None, pix),
        P(exp, pix),
        P(exp, pix),
    )
    return jax.shard_map(
        body,
        mesh=fine,
        in_specs=placed,
        out_specs=(P(exp, pix), P(exp, pix)),
        check_vma=False,
    )
```

```python
import functools
import math

import jax
import jax.numpy as jnp
from jax import lax
from jax.experimental import pallas as pl
from jax.experimental.pallas import tpu as pltpu
from jax.sharding import Mesh
from jax.sharding import PartitionSpec as P

TILE = 128
BF16, F32, I16, I32 = jnp.bfloat16, jnp.float32, jnp.int16, jnp.int32
BASE, RUNG_BITS, LARGEST = 14, (64, 32, 16, 8, 4, 2, 1), 32767.0


def partner(value, axis, flip):
    return lax.ppermute(value, axis, [(i, i ^ flip) for i in range(lax.axis_size(axis))])


def in_hbm(value):
    return pltpu.with_memory_space_constraint(value, pltpu.HBM)


def block_of(ref, which, count):
    return ref[pl.ds(pl.multiple_of(which * count, count), count), :]


def fused_kernel(
    trans_ref, ivar_ref, mask_ref, tangent_ref, coef_ref, full_ref, basis_ref,
    own_ref, other_ref, term_ref, coef_p_ref, coef_t_ref,
):
    step = pl.program_id(0)

    @pl.when(step == 0)
    def _():
        rank = coef_ref.shape[1]
        take = lax.broadcasted_iota(I32, (rank, rank), 0)
        place = lax.broadcasted_iota(I32, (rank, rank), 1)
        low, mid, high = place & 7, place & 112, ((place >> 3) & 1) * 128 + ((place >> 7) & 1) * 8
        chosen = (take == low + mid + high).astype(BF16)
        coef = coef_ref[...]
        coef_p_ref[...] = jnp.dot(coef, chosen, preferred_element_type=F32).astype(BF16)
        coef_t_ref[...] = lax.dot_general(
            chosen, coef, (((0,), (1,)), ((), ())), preferred_element_type=F32
        ).astype(BF16)

    tiles = trans_ref.shape[1] // TILE
    moved = lax.dot_general(
        tangent_ref[...], basis_ref[...], (((0,), (0,)), ((), ())), preferred_element_type=F32
    ) + jnp.dot(coef_p_ref[...], full_ref[...], preferred_element_type=F32)
    mask = mask_ref[...].astype(F32).T
    lanes = lax.broadcasted_iota(I32, mask.shape, 1)
    parts = []
    for t in range(tiles):
        part = slice(t * TILE, (t + 1) * TILE)
        column = jnp.sum(jnp.where(lanes == step * tiles + t, mask, 0.0), axis=1, keepdims=True)
        trans = trans_ref[:, part].astype(F32)
        weights = trans * trans * ivar_ref[:, part].astype(F32) * column
        parts.append((weights * moved[:, part]).astype(BF16))
    weighted = jnp.concatenate(parts, axis=1)

    half = own_ref.shape[0]
    core = lax.axis_index("c")
    for out, which in ((own_ref, core), (other_ref, 1 - core)):
        rows = block_of(coef_t_ref, which, half)
        out[...] = jnp.dot(rows, weighted, preferred_element_type=F32)
    term = lax.dot_general(
        basis_ref[...], weighted, (((1,), (1,)), ((), ())), preferred_element_type=F32
    )

    @pl.when(step == 0)
    def _():
        term_ref[...] = term

    @pl.when(step > 0)
    def _():
        term_ref[...] += term


def encode(total, out_ref):
    cols = total.shape[1]
    largest = jnp.max(jnp.abs(total), axis=1, keepdims=True) * 2.0**-BASE
    scale = jnp.full_like(largest, 2.0**-BASE)
    rung = jnp.zeros_like(largest)
    for bit in RUNG_BITS:
        fits = largest * 2.0**bit <= LARGEST
        largest = jnp.where(fits, largest * 2.0**bit, largest)
        scale = jnp.where(fits, scale * 2.0**bit, scale)
        rung = jnp.where(fits, rung + bit, rung)
    out_ref[:, :cols] = jnp.round(total * scale).astype(I32).astype(I16)
    rungs = jnp.broadcast_to(rung, (total.shape[0], TILE))
    out_ref[:, cols:] = rungs.astype(I32).astype(I16)


def decode(code_ref):
    cols = code_ref.shape[1] - TILE
    rung = code_ref[:, cols:].astype(I32)
    inverse = jnp.full(rung.shape, 2.0**BASE, F32)
    for bit in RUNG_BITS:
        inverse = inverse * jnp.where((rung & bit) != 0, F32(2.0**-bit), F32(1.0))
    return jnp.concatenate(
        [
            code_ref[:, t * TILE : (t + 1) * TILE].astype(I32).astype(F32) * inverse
            for t in range(cols // TILE)
        ],
        axis=1,
    )


def spread_kernel(in_ref, out_ref):
    for i in range(out_ref.shape[0]):
        out_ref[i] = in_ref[...]


def spread_pair_kernel(mine_ref, other_ref, out_ref):
    mine, other = mine_ref[...].astype(F32), other_ref[...].astype(F32)
    first = lax.axis_index("yh") == 0
    pair = [jnp.where(first, mine, other), jnp.where(first, other, mine)]
    pair = jnp.concatenate(pair, axis=0).astype(BF16)
    for i in range(out_ref.shape[0]):
        out_ref[i] = pair


def pack_kernel(term_ref, other_ref, term_codes_ref, other_codes_ref):
    encode(term_ref[...], term_codes_ref)
    encode(other_ref[...], other_codes_ref)


def add_kernel(own_ref, both_ref, out_ref):
    n = own_ref.shape[0]
    came = pl.ds(pl.multiple_of((1 - lax.axis_index("c")) * n, n), n)
    encode(own_ref[...] + decode(both_ref.at[came]), out_ref)


def part_of(ref, i, count):
    return ref.at[i * count : (i + 1) * count]


def halve_kernel(in_ref, keep_ref, give_ref):
    n = keep_ref.shape[0]
    total = sum(decode(part_of(in_ref, i, 2 * n)) for i in range(in_ref.shape[0] // (2 * n)))
    first = lax.axis_index("yh") == 0
    low, high = total[:n], total[n:]
    keep_ref[...] = jnp.where(first, low, high)
    encode(jnp.where(first, high, low), give_ref)


def last_kernel(divisors, terms_ref, mine_ref, came_ref, coef_ref, basis_ref):
    n = coef_ref.shape[0]
    total = sum(decode(part_of(terms_ref, i, n)) for i in range(terms_ref.shape[0] // n))
    coef_ref[...] = total * (1.0 / divisors[0])
    basis_ref[...] = (mine_ref[...] + decode(came_ref)) * (1.0 / divisors[1])


def body(transmission, inverse_var, pixel_mask, coef, basis, coef_tangent, basis_tangent):
    rows, cols = transmission.shape
    rank = basis.shape[0]
    half, mine, ours = rank // 2, rank // 32, rank // 16
    exposures, pixels = rows * 32, cols * 16

    small = lambda kernel, *shapes: pl.pallas_call(
        kernel,
        out_shape=[jax.ShapeDtypeStruct(*shape) for shape in shapes],
        compiler_params=pltpu.CompilerParams(vmem_limit_bytes=8 << 20),
    )
    exchange = lambda value, axis: lax.all_to_all(value, axis, 0, 0, tiled=True)

    across = partner(basis_tangent, "yh", 1)
    [tangent] = small(spread_kernel, ((16, ours, rows), BF16))(coef_tangent.T)
    tangent = exchange(tangent, ("x", "yl")).reshape(rank, rows)
    across, tangent = lax.optimization_barrier((across, tangent))

    [pair] = small(spread_pair_kernel, ((8, 2 * mine, cols), BF16))(in_hbm(basis_tangent), across)
    arrived = exchange(pair, "z").reshape(half, cols)
    full = lax.all_gather(arrived, "c", axis=0, tiled=True)

    width = cols // 2
    whole = lambda *shape: pl.BlockSpec(shape, lambda i: (0,) * len(shape))
    tall = lambda n: pl.BlockSpec((n, width), lambda i: (0, i))
    own, other, term = pl.pallas_call(
        fused_kernel,
        grid=(cols // width,),
        in_specs=[
            tall(rows), tall(rows), whole(cols // TILE, rows), whole(rank, rows),
            whole(rows, rank), tall(rank), tall(rank),
        ],
        out_specs=[tall(half), tall(half), whole(rank, rows)],
        out_shape=[
            jax.ShapeDtypeStruct((half, cols), F32),
            jax.ShapeDtypeStruct((half, cols), F32),
            jax.ShapeDtypeStruct((rank, rows), F32),
        ],
        scratch_shapes=[pltpu.VMEM((rows, rank), BF16), pltpu.VMEM((rank, rows), BF16)],
        compiler_params=pltpu.CompilerParams(vmem_limit_bytes=16 << 20),
        cost_estimate=pl.CostEstimate(
            flops=8 * rows * cols * rank, bytes_accessed=6 * rows * cols, transcendentals=0
        ),
    )(transmission, inverse_var, pixel_mask.T, tangent, in_hbm(coef), full, in_hbm(basis))

    terms, codes = small(
        pack_kernel, ((rank, rows + TILE), I16), ((half, cols + TILE), I16)
    )(term, other)
    codes = lax.all_gather(codes, "c", axis=0, tiled=True)
    [codes] = small(add_kernel, ((half, cols + TILE), I16))(own, codes)
    codes = exchange(codes.reshape(8, 2 * mine, cols + TILE), "z").reshape(half, cols + TILE)
    codes, terms = lax.optimization_barrier((codes, terms))

    keep, give = small(halve_kernel, ((mine, cols), F32), ((mine, cols + TILE), I16))(codes)
    came = partner(give, "yh", 1)
    terms = exchange(terms.reshape(16, ours, rows + TILE), ("x", "yl")).reshape(rank, rows + TILE)
    coef_grad, basis_grad = small(
        functools.partial(last_kernel, (math.sqrt(pixels), math.sqrt(exposures))),
        ((ours, rows), F32),
        ((mine, cols), F32),
    )(terms, keep, came)
    return (coef_grad.T, basis_grad)


def solution(mesh):
    fine = Mesh(mesh.devices.reshape(2, 8, 2, 4, 4), ("yh", "z", "c", "x", "yl"))
    exp, pix = ("yh", "z", "c"), ("x", "yl")
    placed = (
        P(exp, pix),
        P(exp, pix),
        P(exp, pix),
        P(exp, None),
        P(None, pix),
        P(exp, pix),
        P(exp, pix),
    )
    return jax.shard_map(
        body,
        mesh=fine,
        in_specs=placed,
        out_specs=(P(exp, pix), P(exp, pix)),
        check_vma=False,
    )
```

```python
import functools
import math

import jax
import jax.numpy as jnp
from jax import lax
from jax.experimental import pallas as pl
from jax.experimental.pallas import tpu as pltpu
from jax.sharding import Mesh
from jax.sharding import PartitionSpec as P

TILE = 128
BF16, F32, I16, I32 = jnp.bfloat16, jnp.float32, jnp.int16, jnp.int32
BASE, RUNG_BITS, LARGEST = 14, (64, 32, 16, 8, 4, 2, 1), 32767.0


def partner(value, axis, flip):
    return lax.ppermute(value, axis, [(i, i ^ flip) for i in range(lax.axis_size(axis))])


def in_hbm(value):
    return pltpu.with_memory_space_constraint(value, pltpu.HBM)


def block_of(ref, which, count):
    return ref[pl.ds(pl.multiple_of(which * count, count), count), :]


def fused_kernel(
    trans_ref, ivar_ref, mask_ref, tangent_ref, coef_ref, full_ref, basis_ref,
    own_ref, other_ref, weighted_ref, coef_p_ref, coef_t_ref,
):
    step = pl.program_id(0)

    @pl.when(step == 0)
    def _():
        rank = coef_ref.shape[1]
        take = lax.broadcasted_iota(I32, (rank, rank), 0)
        place = lax.broadcasted_iota(I32, (rank, rank), 1)
        low, mid, high = place & 7, place & 112, ((place >> 3) & 1) * 128 + ((place >> 7) & 1) * 8
        chosen = (take == low + mid + high).astype(BF16)
        coef = coef_ref[...]
        coef_p_ref[...] = jnp.dot(coef, chosen, preferred_element_type=F32).astype(BF16)
        coef_t_ref[...] = lax.dot_general(
            chosen, coef, (((0,), (1,)), ((), ())), preferred_element_type=F32
        ).astype(BF16)

    tiles = trans_ref.shape[1] // TILE
    moved = lax.dot_general(
        tangent_ref[...], basis_ref[...], (((0,), (0,)), ((), ())), preferred_element_type=F32
    ) + jnp.dot(coef_p_ref[...], full_ref[...], preferred_element_type=F32)
    mask = mask_ref[...].astype(F32).T
    lanes = lax.broadcasted_iota(I32, mask.shape, 1)
    parts = []
    for t in range(tiles):
        part = slice(t * TILE, (t + 1) * TILE)
        column = jnp.sum(jnp.where(lanes == step * tiles + t, mask, 0.0), axis=1, keepdims=True)
        trans = trans_ref[:, part].astype(F32)
        weights = trans * trans * ivar_ref[:, part].astype(F32) * column
        parts.append((weights * moved[:, part]).astype(BF16))
    weighted = jnp.concatenate(parts, axis=1)
    weighted_ref[...] = weighted

    half = own_ref.shape[0]
    core = lax.axis_index("c")
    for out, which in ((own_ref, core), (other_ref, 1 - core)):
        rows = block_of(coef_t_ref, which, half)
        out[...] = jnp.dot(rows, weighted, preferred_element_type=F32)


def encode(total, out_ref):
    cols = total.shape[1]
    largest = jnp.max(jnp.abs(total), axis=1, keepdims=True) * 2.0**-BASE
    scale = jnp.full_like(largest, 2.0**-BASE)
    rung = jnp.zeros_like(largest)
    for bit in RUNG_BITS:
        fits = largest * 2.0**bit <= LARGEST
        largest = jnp.where(fits, largest * 2.0**bit, largest)
        scale = jnp.where(fits, scale * 2.0**bit, scale)
        rung = jnp.where(fits, rung + bit, rung)
    out_ref[:, :cols] = jnp.round(total * scale).astype(I32).astype(I16)
    rungs = jnp.broadcast_to(rung, (total.shape[0], TILE))
    out_ref[:, cols:] = rungs.astype(I32).astype(I16)


def decode(code_ref):
    cols = code_ref.shape[1] - TILE
    rung = code_ref[:, cols:].astype(I32)
    inverse = jnp.full(rung.shape, 2.0**BASE, F32)
    for bit in RUNG_BITS:
        inverse = inverse * jnp.where((rung & bit) != 0, F32(2.0**-bit), F32(1.0))
    return jnp.concatenate(
        [
            code_ref[:, t * TILE : (t + 1) * TILE].astype(I32).astype(F32) * inverse
            for t in range(cols // TILE)
        ],
        axis=1,
    )


def spread_kernel(in_ref, out_ref):
    for i in range(out_ref.shape[0]):
        out_ref[i] = in_ref[...]


def spread_pair_kernel(mine_ref, other_ref, out_ref):
    mine, other = mine_ref[...].astype(F32), other_ref[...].astype(F32)
    first = lax.axis_index("yh") == 0
    pair = [jnp.where(first, mine, other), jnp.where(first, other, mine)]
    pair = jnp.concatenate(pair, axis=0).astype(BF16)
    for i in range(out_ref.shape[0]):
        out_ref[i] = pair


def pack_kernel(other_ref, out_ref):
    encode(other_ref[...], out_ref)


def term_kernel(basis_ref, weighted_ref, out_ref):
    term = lax.dot_general(
        basis_ref[...], weighted_ref[...], (((1,), (1,)), ((), ())), preferred_element_type=F32
    )
    encode(term, out_ref)


def add_kernel(own_ref, both_ref, out_ref):
    n = own_ref.shape[0]
    came = pl.ds(pl.multiple_of((1 - lax.axis_index("c")) * n, n), n)
    encode(own_ref[...] + decode(both_ref.at[came]), out_ref)


def part_of(ref, i, count):
    return ref.at[i * count : (i + 1) * count]


def halve_kernel(in_ref, keep_ref, give_ref):
    n = keep_ref.shape[0]
    total = sum(decode(part_of(in_ref, i, 2 * n)) for i in range(in_ref.shape[0] // (2 * n)))
    first = lax.axis_index("yh") == 0
    low, high = total[:n], total[n:]
    keep_ref[...] = jnp.where(first, low, high)
    encode(jnp.where(first, high, low), give_ref)


def last_kernel(divisors, terms_ref, mine_ref, came_ref, coef_ref, basis_ref):
    n = coef_ref.shape[0]
    total = sum(decode(part_of(terms_ref, i, n)) for i in range(terms_ref.shape[0] // n))
    coef_ref[...] = total * (1.0 / divisors[0])
    basis_ref[...] = (mine_ref[...] + decode(came_ref)) * (1.0 / divisors[1])


def body(transmission, inverse_var, pixel_mask, coef, basis, coef_tangent, basis_tangent):
    rows, cols = transmission.shape
    rank = basis.shape[0]
    half, mine, ours = rank // 2, rank // 32, rank // 16
    exposures, pixels = rows * 32, cols * 16

    small = lambda kernel, *shapes: pl.pallas_call(
        kernel,
        out_shape=[jax.ShapeDtypeStruct(*shape) for shape in shapes],
        compiler_params=pltpu.CompilerParams(vmem_limit_bytes=8 << 20),
    )
    exchange = lambda value, axis: lax.all_to_all(value, axis, 0, 0, tiled=True)

    across = partner(basis_tangent, "yh", 1)
    tangent = pl.pallas_call(
        spread_kernel,
        out_shape=pltpu.HBM((16, ours, rows), BF16),
        compiler_params=pltpu.CompilerParams(vmem_limit_bytes=8 << 20),
    )(coef_tangent.T)
    tangent = exchange(tangent, ("x", "yl")).reshape(rank, rows)
    across, tangent = lax.optimization_barrier((across, tangent))

    [pair] = small(spread_pair_kernel, ((8, 2 * mine, cols), BF16))(in_hbm(basis_tangent), across)
    arrived = exchange(pair, "z").reshape(half, cols)
    full = lax.all_gather(arrived, "c", axis=0, tiled=True)

    width = cols // 2
    whole = lambda *shape: pl.BlockSpec(shape, lambda i: (0,) * len(shape))
    tall = lambda n: pl.BlockSpec((n, width), lambda i: (0, i))
    own, other, weighted = pl.pallas_call(
        fused_kernel,
        grid=(cols // width,),
        in_specs=[
            tall(rows), tall(rows), whole(cols // TILE, rows), whole(rank, rows),
            whole(rows, rank), tall(rank), tall(rank),
        ],
        out_specs=[tall(half), tall(half), tall(rows)],
        out_shape=[
            jax.ShapeDtypeStruct((half, cols), F32),
            jax.ShapeDtypeStruct((half, cols), F32),
            pltpu.HBM((rows, cols), BF16),
        ],
        scratch_shapes=[pltpu.VMEM((rows, rank), BF16), pltpu.VMEM((rank, rows), BF16)],
        compiler_params=pltpu.CompilerParams(vmem_limit_bytes=16 << 20),
        cost_estimate=pl.CostEstimate(
            flops=6 * rows * cols * rank, bytes_accessed=6 * rows * cols, transcendentals=0
        ),
    )(transmission, inverse_var, pixel_mask.T, tangent, in_hbm(coef), full, in_hbm(basis))

    [codes] = small(pack_kernel, ((half, cols + TILE), I16))(other)
    codes = lax.all_gather(codes, "c", axis=0, tiled=True)
    [codes] = small(add_kernel, ((half, cols + TILE), I16))(own, codes)
    codes = exchange(codes.reshape(8, 2 * mine, cols + TILE), "z").reshape(half, cols + TILE)
    terms = pl.pallas_call(
        term_kernel,
        out_shape=jax.ShapeDtypeStruct((rank, rows + TILE), I16),
        compiler_params=pltpu.CompilerParams(vmem_limit_bytes=16 << 20),
        cost_estimate=pl.CostEstimate(
            flops=2 * rows * cols * rank, bytes_accessed=4 * rows * cols, transcendentals=0
        ),
    )(in_hbm(basis), in_hbm(weighted))
    codes, terms = lax.optimization_barrier((codes, terms))

    keep, give = small(halve_kernel, ((mine, cols), F32), ((mine, cols + TILE), I16))(codes)
    came = partner(give, "yh", 1)
    terms = exchange(terms.reshape(16, ours, rows + TILE), ("x", "yl")).reshape(rank, rows + TILE)
    coef_grad, basis_grad = small(
        functools.partial(last_kernel, (math.sqrt(pixels), math.sqrt(exposures))),
        ((ours, rows), F32),
        ((mine, cols), F32),
    )(terms, keep, came)
    return (coef_grad.T, basis_grad)


def solution(mesh):
    fine = Mesh(mesh.devices.reshape(2, 8, 2, 4, 4), ("yh", "z", "c", "x", "yl"))
    exp, pix = ("yh", "z", "c"), ("x", "yl")
    placed = (
        P(exp, pix),
        P(exp, pix),
        P(exp, pix),
        P(exp, None),
        P(None, pix),
        P(exp, pix),
        P(exp, pix),
    )
    return jax.shard_map(
        body,
        mesh=fine,
        in_specs=placed,
        out_specs=(P(exp, pix), P(exp, pix)),
        check_vma=False,
    )
```

```python
import functools
import math

import jax
import jax.numpy as jnp
from jax import lax
from jax.experimental import pallas as pl
from jax.experimental.pallas import tpu as pltpu
from jax.sharding import Mesh
from jax.sharding import PartitionSpec as P

TILE = 128
BF16, F32, I16, I32 = jnp.bfloat16, jnp.float32, jnp.int16, jnp.int32
BASE, RUNG_BITS, LARGEST = 14, (64, 32, 16, 8, 4, 2, 1), 32767.0


def partner(value, axis, flip):
    return lax.ppermute(value, axis, [(i, i ^ flip) for i in range(lax.axis_size(axis))])


def in_hbm(value):
    return pltpu.with_memory_space_constraint(value, pltpu.HBM)


def block_of(ref, which, count):
    return ref[pl.ds(pl.multiple_of(which * count, count), count), :]


def fused_kernel(
    trans_ref, ivar_ref, mask_ref, tangent_ref, coef_ref, full_ref, basis_ref,
    own_ref, other_ref, term_ref, coef_p_ref, coef_t_ref,
):
    step = pl.program_id(0)

    @pl.when(step == 0)
    def _():
        rank = coef_ref.shape[1]
        take = lax.broadcasted_iota(I32, (rank, rank), 0)
        place = lax.broadcasted_iota(I32, (rank, rank), 1)
        low, mid, high = place & 7, place & 112, ((place >> 3) & 1) * 128 + ((place >> 7) & 1) * 8
        chosen = (take == low + mid + high).astype(BF16)
        coef = coef_ref[...]
        coef_p_ref[...] = jnp.dot(coef, chosen, preferred_element_type=F32).astype(BF16)
        coef_t_ref[...] = lax.dot_general(
            chosen, coef, (((0,), (1,)), ((), ())), preferred_element_type=F32
        ).astype(BF16)

    tiles = trans_ref.shape[1] // TILE
    moved = lax.dot_general(
        tangent_ref[...], basis_ref[...], (((0,), (0,)), ((), ())), preferred_element_type=F32
    ) + jnp.dot(coef_p_ref[...], full_ref[...], preferred_element_type=F32)
    mask = mask_ref[...].astype(F32).T
    lanes = lax.broadcasted_iota(I32, mask.shape, 1)
    parts = []
    for t in range(tiles):
        part = slice(t * TILE, (t + 1) * TILE)
        column = jnp.sum(jnp.where(lanes == step * tiles + t, mask, 0.0), axis=1, keepdims=True)
        trans = trans_ref[:, part].astype(F32)
        weights = trans * trans * ivar_ref[:, part].astype(F32) * column
        parts.append((weights * moved[:, part]).astype(BF16))
    weighted = jnp.concatenate(parts, axis=1)

    half = own_ref.shape[0]
    core = lax.axis_index("c")
    for out, which in ((own_ref, core), (other_ref, 1 - core)):
        rows = block_of(coef_t_ref, which, half)
        out[...] = jnp.dot(rows, weighted, preferred_element_type=F32)
    term = lax.dot_general(
        basis_ref[...], weighted, (((1,), (1,)), ((), ())), preferred_element_type=F32
    )

    @pl.when(step == 0)
    def _():
        term_ref[...] = term

    @pl.when(step > 0)
    def _():
        term_ref[...] += term


def encode(total, out_ref):
    cols = total.shape[1]
    largest = jnp.max(jnp.abs(total), axis=1, keepdims=True) * 2.0**-BASE
    scale = jnp.full_like(largest, 2.0**-BASE)
    rung = jnp.zeros_like(largest)
    for bit in RUNG_BITS:
        fits = largest * 2.0**bit <= LARGEST
        largest = jnp.where(fits, largest * 2.0**bit, largest)
        scale = jnp.where(fits, scale * 2.0**bit, scale)
        rung = jnp.where(fits, rung + bit, rung)
    out_ref[:, :cols] = jnp.round(total * scale).astype(I32).astype(I16)
    rungs = jnp.broadcast_to(rung, (total.shape[0], TILE))
    out_ref[:, cols:] = rungs.astype(I32).astype(I16)


def decode(code_ref):
    cols = code_ref.shape[1] - TILE
    rung = code_ref[:, cols:].astype(I32)
    inverse = jnp.full(rung.shape, 2.0**BASE, F32)
    for bit in RUNG_BITS:
        inverse = inverse * jnp.where((rung & bit) != 0, F32(2.0**-bit), F32(1.0))
    return jnp.concatenate(
        [
            code_ref[:, t * TILE : (t + 1) * TILE].astype(I32).astype(F32) * inverse
            for t in range(cols // TILE)
        ],
        axis=1,
    )


def spread_kernel(in_ref, out_ref):
    for i in range(out_ref.shape[0]):
        out_ref[i] = in_ref[...]


def spread_pair_kernel(mine_ref, other_ref, out_ref):
    mine, other = mine_ref[...].astype(F32), other_ref[...].astype(F32)
    first = lax.axis_index("yh") == 0
    pair = [jnp.where(first, mine, other), jnp.where(first, other, mine)]
    pair = jnp.concatenate(pair, axis=0).astype(BF16)
    for i in range(out_ref.shape[0]):
        out_ref[i] = pair


def pack_kernel(term_ref, other_ref, term_codes_ref, other_codes_ref):
    encode(term_ref[...], term_codes_ref)
    encode(other_ref[...], other_codes_ref)


def add_kernel(own_ref, both_ref, out_ref):
    n = own_ref.shape[0]
    came = pl.ds(pl.multiple_of((1 - lax.axis_index("c")) * n, n), n)
    encode(own_ref[...] + decode(both_ref.at[came]), out_ref)


def part_of(ref, i, count):
    return ref.at[i * count : (i + 1) * count]


def halve_kernel(in_ref, keep_ref, give_ref):
    n = keep_ref.shape[0]
    total = sum(decode(part_of(in_ref, i, 2 * n)) for i in range(in_ref.shape[0] // (2 * n)))
    first = lax.axis_index("yh") == 0
    low, high = total[:n], total[n:]
    keep_ref[...] = jnp.where(first, low, high)
    encode(jnp.where(first, high, low), give_ref)


def last_kernel(divisors, terms_ref, mine_ref, came_ref, coef_ref, basis_ref):
    n = coef_ref.shape[0]
    total = sum(decode(part_of(terms_ref, i, n)) for i in range(terms_ref.shape[0] // n))
    coef_ref[...] = total * (1.0 / divisors[0])
    basis_ref[...] = (mine_ref[...] + decode(came_ref)) * (1.0 / divisors[1])


def body(transmission, inverse_var, pixel_mask, coef, basis, coef_tangent, basis_tangent):
    rows, cols = transmission.shape
    rank = basis.shape[0]
    half, mine, ours = rank // 2, rank // 32, rank // 16
    exposures, pixels = rows * 32, cols * 16

    small = lambda kernel, *shapes: pl.pallas_call(
        kernel,
        out_shape=[jax.ShapeDtypeStruct(*shape) for shape in shapes],
        compiler_params=pltpu.CompilerParams(vmem_limit_bytes=8 << 20),
    )
    exchange = lambda value, axis: lax.all_to_all(value, axis, 0, 0, tiled=True)

    across = partner(basis_tangent, "yh", 1)
    [tangent] = small(spread_kernel, ((16, ours, rows), BF16))(coef_tangent.T)
    tangent = exchange(tangent, ("x", "yl")).reshape(rank, rows)
    across, tangent = lax.optimization_barrier((across, tangent))

    [pair] = small(spread_pair_kernel, ((8, 2 * mine, cols), BF16))(in_hbm(basis_tangent), across)
    arrived = exchange(pair, "z").reshape(half, cols)
    full = lax.all_gather(arrived, "c", axis=0, tiled=True)

    width = cols
    whole = lambda *shape: pl.BlockSpec(shape, lambda i: (0,) * len(shape))
    tall = lambda n: pl.BlockSpec((n, width), lambda i: (0, i))
    own, other, term = pl.pallas_call(
        fused_kernel,
        grid=(cols // width,),
        in_specs=[
            tall(rows), tall(rows), whole(cols // TILE, rows), whole(rank, rows),
            whole(rows, rank), tall(rank), tall(rank),
        ],
        out_specs=[tall(half), tall(half), whole(rank, rows)],
        out_shape=[
            jax.ShapeDtypeStruct((half, cols), F32),
            jax.ShapeDtypeStruct((half, cols), F32),
            jax.ShapeDtypeStruct((rank, rows), F32),
        ],
        scratch_shapes=[pltpu.VMEM((rows, rank), BF16), pltpu.VMEM((rank, rows), BF16)],
        compiler_params=pltpu.CompilerParams(vmem_limit_bytes=24 << 20),
        cost_estimate=pl.CostEstimate(
            flops=8 * rows * cols * rank, bytes_accessed=6 * rows * cols, transcendentals=0
        ),
    )(transmission, inverse_var, pixel_mask.T, tangent, in_hbm(coef), full, in_hbm(basis))

    terms, codes = small(
        pack_kernel, ((rank, rows + TILE), I16), ((half, cols + TILE), I16)
    )(term, other)
    codes = lax.all_gather(codes, "c", axis=0, tiled=True)
    [codes] = small(add_kernel, ((half, cols + TILE), I16))(own, codes)
    codes = exchange(codes.reshape(8, 2 * mine, cols + TILE), "z").reshape(half, cols + TILE)
    codes, terms = lax.optimization_barrier((codes, terms))

    keep, give = small(halve_kernel, ((mine, cols), F32), ((mine, cols + TILE), I16))(codes)
    came = partner(give, "yh", 1)
    terms = exchange(terms.reshape(16, ours, rows + TILE), ("x", "yl")).reshape(rank, rows + TILE)
    coef_grad, basis_grad = small(
        functools.partial(last_kernel, (math.sqrt(pixels), math.sqrt(exposures))),
        ((ours, rows), F32),
        ((mine, cols), F32),
    )(terms, keep, came)
    return (coef_grad.T, basis_grad)


def solution(mesh):
    fine = Mesh(mesh.devices.reshape(2, 8, 2, 4, 4), ("yh", "z", "c", "x", "yl"))
    exp, pix = ("yh", "z", "c"), ("x", "yl")
    placed = (
        P(exp, pix),
        P(exp, pix),
        P(exp, pix),
        P(exp, None),
        P(None, pix),
        P(exp, pix),
        P(exp, pix),
    )
    return jax.shard_map(
        body,
        mesh=fine,
        in_specs=placed,
        out_specs=(P(exp, pix), P(exp, pix)),
        check_vma=False,
    )
```

```python
import functools
import math

import jax
import jax.numpy as jnp
from jax import lax
from jax.experimental import pallas as pl
from jax.experimental.pallas import tpu as pltpu
from jax.sharding import Mesh
from jax.sharding import PartitionSpec as P

TILE = 128
BF16, F32, I16, I32 = jnp.bfloat16, jnp.float32, jnp.int16, jnp.int32
BASE, RUNG_BITS, LARGEST = 14, (64, 32, 16, 8, 4, 2, 1), 32767.0


def partner(value, axis, flip):
    return lax.ppermute(value, axis, [(i, i ^ flip) for i in range(lax.axis_size(axis))])


def in_hbm(value):
    return pltpu.with_memory_space_constraint(value, pltpu.HBM)


def block_of(ref, which, count):
    return ref[pl.ds(pl.multiple_of(which * count, count), count), :]


def fused_kernel(
    trans_ref, ivar_ref, mask_ref, tangent_ref, coef_ref, full_ref, basis_ref,
    own_ref, other_codes_ref, term_codes_ref, coef_p_ref, coef_t_ref,
):
    step = pl.program_id(0)

    @pl.when(step == 0)
    def _():
        rank = coef_ref.shape[1]
        take = lax.broadcasted_iota(I32, (rank, rank), 0)
        place = lax.broadcasted_iota(I32, (rank, rank), 1)
        low, mid, high = place & 7, place & 112, ((place >> 3) & 1) * 128 + ((place >> 7) & 1) * 8
        chosen = (take == low + mid + high).astype(BF16)
        coef = coef_ref[...]
        coef_p_ref[...] = jnp.dot(coef, chosen, preferred_element_type=F32).astype(BF16)
        coef_t_ref[...] = lax.dot_general(
            chosen, coef, (((0,), (1,)), ((), ())), preferred_element_type=F32
        ).astype(BF16)

    tiles = trans_ref.shape[1] // TILE
    moved = lax.dot_general(
        tangent_ref[...], basis_ref[...], (((0,), (0,)), ((), ())), preferred_element_type=F32
    ) + jnp.dot(coef_p_ref[...], full_ref[...], preferred_element_type=F32)
    mask = mask_ref[...].astype(F32).T
    lanes = lax.broadcasted_iota(I32, mask.shape, 1)
    parts = []
    for t in range(tiles):
        part = slice(t * TILE, (t + 1) * TILE)
        column = jnp.sum(jnp.where(lanes == step * tiles + t, mask, 0.0), axis=1, keepdims=True)
        trans = trans_ref[:, part].astype(F32)
        weights = trans * trans * ivar_ref[:, part].astype(F32) * column
        parts.append((weights * moved[:, part]).astype(BF16))
    weighted = jnp.concatenate(parts, axis=1)

    half = own_ref.shape[0]
    core = lax.axis_index("c")
    own_ref[...] = jnp.dot(
        block_of(coef_t_ref, core, half), weighted, preferred_element_type=F32
    )
    other = jnp.dot(block_of(coef_t_ref, 1 - core, half), weighted, preferred_element_type=F32)
    encode(other, other_codes_ref)
    term = lax.dot_general(
        basis_ref[...], weighted, (((1,), (1,)), ((), ())), preferred_element_type=F32
    )
    encode(term, term_codes_ref)


def encode(total, out_ref):
    cols = total.shape[1]
    largest = jnp.max(jnp.abs(total), axis=1, keepdims=True) * 2.0**-BASE
    scale = jnp.full_like(largest, 2.0**-BASE)
    rung = jnp.zeros_like(largest)
    for bit in RUNG_BITS:
        fits = largest * 2.0**bit <= LARGEST
        largest = jnp.where(fits, largest * 2.0**bit, largest)
        scale = jnp.where(fits, scale * 2.0**bit, scale)
        rung = jnp.where(fits, rung + bit, rung)
    out_ref[:, :cols] = jnp.round(total * scale).astype(I32).astype(I16)
    rungs = jnp.broadcast_to(rung, (total.shape[0], TILE))
    out_ref[:, cols:] = rungs.astype(I32).astype(I16)


def decode(code_ref):
    cols = code_ref.shape[1] - TILE
    rung = code_ref[:, cols:].astype(I32)
    inverse = jnp.full(rung.shape, 2.0**BASE, F32)
    for bit in RUNG_BITS:
        inverse = inverse * jnp.where((rung & bit) != 0, F32(2.0**-bit), F32(1.0))
    return jnp.concatenate(
        [
            code_ref[:, t * TILE : (t + 1) * TILE].astype(I32).astype(F32) * inverse
            for t in range(cols // TILE)
        ],
        axis=1,
    )


def spread_kernel(in_ref, out_ref):
    for i in range(out_ref.shape[0]):
        out_ref[i] = in_ref[...]


def spread_pair_kernel(mine_ref, other_ref, out_ref):
    mine, other = mine_ref[...].astype(F32), other_ref[...].astype(F32)
    first = lax.axis_index("yh") == 0
    pair = [jnp.where(first, mine, other), jnp.where(first, other, mine)]
    pair = jnp.concatenate(pair, axis=0).astype(BF16)
    for i in range(out_ref.shape[0]):
        out_ref[i] = pair


def add_kernel(own_ref, both_ref, out_ref):
    n = own_ref.shape[0]
    came = pl.ds(pl.multiple_of((1 - lax.axis_index("c")) * n, n), n)
    encode(own_ref[...] + decode(both_ref.at[came]), out_ref)


def part_of(ref, i, count):
    return ref.at[i * count : (i + 1) * count]


def halve_kernel(in_ref, keep_ref, give_ref):
    n = keep_ref.shape[0]
    total = sum(decode(part_of(in_ref, i, 2 * n)) for i in range(in_ref.shape[0] // (2 * n)))
    first = lax.axis_index("yh") == 0
    low, high = total[:n], total[n:]
    keep_ref[...] = jnp.where(first, low, high)
    encode(jnp.where(first, high, low), give_ref)


def last_kernel(divisors, terms_ref, mine_ref, came_ref, coef_ref, basis_ref):
    n = coef_ref.shape[0]
    total = sum(decode(part_of(terms_ref, i, n)) for i in range(terms_ref.shape[0] // n))
    coef_ref[...] = total * (1.0 / divisors[0])
    basis_ref[...] = (mine_ref[...] + decode(came_ref)) * (1.0 / divisors[1])


def body(transmission, inverse_var, pixel_mask, coef, basis, coef_tangent, basis_tangent):
    rows, cols = transmission.shape
    rank = basis.shape[0]
    half, mine, ours = rank // 2, rank // 32, rank // 16
    exposures, pixels = rows * 32, cols * 16

    small = lambda kernel, *shapes: pl.pallas_call(
        kernel,
        out_shape=[jax.ShapeDtypeStruct(*shape) for shape in shapes],
        compiler_params=pltpu.CompilerParams(vmem_limit_bytes=8 << 20),
    )
    exchange = lambda value, axis: lax.all_to_all(value, axis, 0, 0, tiled=True)

    across = partner(basis_tangent, "yh", 1)
    [tangent] = small(spread_kernel, ((16, ours, rows), BF16))(coef_tangent.T)
    tangent = exchange(tangent, ("x", "yl")).reshape(rank, rows)
    across, tangent = lax.optimization_barrier((across, tangent))

    [pair] = small(spread_pair_kernel, ((8, 2 * mine, cols), BF16))(in_hbm(basis_tangent), across)
    arrived = exchange(pair, "z").reshape(half, cols)
    full = lax.all_gather(arrived, "c", axis=0, tiled=True)

    width = cols
    whole = lambda *shape: pl.BlockSpec(shape, lambda i: (0,) * len(shape))
    tall = lambda n: pl.BlockSpec((n, width), lambda i: (0, i))
    own, codes, terms = pl.pallas_call(
        fused_kernel,
        grid=(cols // width,),
        in_specs=[
            tall(rows), tall(rows), whole(cols // TILE, rows), whole(rank, rows),
            whole(rows, rank), tall(rank), tall(rank),
        ],
        out_specs=[tall(half), whole(half, cols + TILE), whole(rank, rows + TILE)],
        out_shape=[
            jax.ShapeDtypeStruct((half, cols), F32),
            jax.ShapeDtypeStruct((half, cols + TILE), I16),
            jax.ShapeDtypeStruct((rank, rows + TILE), I16),
        ],
        scratch_shapes=[pltpu.VMEM((rows, rank), BF16), pltpu.VMEM((rank, rows), BF16)],
        compiler_params=pltpu.CompilerParams(vmem_limit_bytes=24 << 20),
        cost_estimate=pl.CostEstimate(
            flops=8 * rows * cols * rank, bytes_accessed=6 * rows * cols, transcendentals=0
        ),
    )(transmission, inverse_var, pixel_mask.T, tangent, in_hbm(coef), full, in_hbm(basis))

    codes = lax.all_gather(codes, "c", axis=0, tiled=True)
    [codes] = small(add_kernel, ((half, cols + TILE), I16))(own, codes)
    codes = exchange(codes.reshape(8, 2 * mine, cols + TILE), "z").reshape(half, cols + TILE)
    codes, terms = lax.optimization_barrier((codes, terms))

    keep, give = small(halve_kernel, ((mine, cols), F32), ((mine, cols + TILE), I16))(codes)
    came = partner(give, "yh", 1)
    terms = exchange(terms.reshape(16, ours, rows + TILE), ("x", "yl")).reshape(rank, rows + TILE)
    coef_grad, basis_grad = small(
        functools.partial(last_kernel, (math.sqrt(pixels), math.sqrt(exposures))),
        ((ours, rows), F32),
        ((mine, cols), F32),
    )(terms, keep, came)
    return (coef_grad.T, basis_grad)


def solution(mesh):
    fine = Mesh(mesh.devices.reshape(2, 8, 2, 4, 4), ("yh", "z", "c", "x", "yl"))
    exp, pix = ("yh", "z", "c"), ("x", "yl")
    placed = (
        P(exp, pix),
        P(exp, pix),
        P(exp, pix),
        P(exp, None),
        P(None, pix),
        P(exp, pix),
        P(exp, pix),
    )
    return jax.shard_map(
        body,
        mesh=fine,
        in_specs=placed,
        out_specs=(P(exp, pix), P(exp, pix)),
        check_vma=False,
    )
```
